32 devices in a mesh: dp: 16 (over z, y, core), mp: 2 (over x).
Axes of the slice: x: 2, y: 2, z: 4, core: 2. Of those that a mesh axis runs over, the one named last changes fastest.
Arguments:
- layer_in: bfloat16 [16, 1024, 1024], P('dp', 'mp'), may hold values from -6 to 6
- seg_ids: int32 [16, 1024], P('dp'), may hold values from 0 to 5, as said below
- pad_mask: int32 [16, 1024], P('dp'), may hold values from 0 to 1, as said below
- wq: bfloat16 [1024, 1024], P(None, 'mp'), may hold values from -0.375 to 0.375
- wk: bfloat16 [1024, 1024], P(None, 'mp'), may hold values from -0.1875 to 0.1875
- wv: bfloat16 [1024, 1024], P(None, 'mp'), may hold values from -0.1875 to 0.1875
- wo: bfloat16 [1024, 1024], P('mp'), may hold values from -1.5 to 1.5
- wi0: bfloat16 [1024, 2816], P(None, 'mp'), may hold values from -0.1875 to 0.1875
- wi1: bfloat16 [1024, 2816], P(None, 'mp'), may hold values from -0.1875 to 0.1875
- wf: bfloat16 [2816, 1024], P('mp'), may hold values from -0.109375 to 0.109375
- gain_attn: float32 [1024], replicated, may hold values from 0.5 to 1.5
- gain_ffn: float32 [1024], replicated, may hold values from 0.5 to 1.5
- out_grad: bfloat16 [16, 1024, 1024], P('dp', 'mp'), may hold values from -6 to 6
Outputs:
- layer_out: bfloat16 [16, 1024, 1024], P('dp', 'mp')
- d_x: float32 [16, 1024, 1024], P('dp', 'mp')
- d_wq: float32 [1024, 1024], P('dp', 'mp')
- d_wk: float32 [1024, 1024], P('dp', 'mp')
- d_wv: float32 [1024, 1024], P('dp', 'mp')
- d_wo: float32 [1024, 1024], P('mp', 'dp')
- d_wi0: float32 [1024, 2816], P('dp', 'mp')
- d_wi1: float32 [1024, 2816], P('dp', 'mp')
- d_wf: float32 [2816, 1024], P('mp', 'dp')
- d_gain_attn: float32 [1024], replicated
- d_gain_ffn: float32 [1024], replicated
The draws below stay inside these ranges and needn't reach their ends.
Inputs may be any that keep to these rules, and one draw needn't show every extreme that they name: `seg_ids`: segment ids never fall along a row. `pad_mask`: each row is 1 up to some position and 0 after it.
All inputs are finite; a program needn't handle non-finite values.
Results may differ from the reference program's by a relative error of at most 0.022.
Values may be sent and summed in bfloat16 or wider, within the bound.
No kernel may reach another device: no remote copies, remote signals or barrier semaphores. Data moves between devices by JAX's collectives and lax.ppermute only.
A program may use at most 192 MiB of HBM per device.

```python
import jax
import jax.numpy as jnp
from jax import lax

D = 1024
H = 16
HD = 64
FF = 2816
SEQ = 1024
ROWS = 16


def segment_layout(key):
    splits = jax.random.split(key, 5)
    seq_len = SEQ
    long_start = jax.random.randint(splits[0], (ROWS, 1), 1, seq_len // 8)
    lead_start = jax.random.randint(splits[1], (ROWS, 1), 0, long_start)
    long_end = jax.random.randint(splits[2], (ROWS, 1), 7 * seq_len // 8, 15 * seq_len // 16)
    pad_start = seq_len - jax.random.randint(splits[3], (ROWS, 1), 0, seq_len // 16)
    tail_start = jax.random.randint(splits[4], (ROWS, 1), long_end, pad_start + 1)
    position = jnp.arange(seq_len, dtype=jnp.int32)[None, :]
    ids_total = (position >= lead_start).astype(jnp.int32) + (position >= long_start).astype(jnp.int32)
    ids_total = ids_total + (position >= long_end).astype(jnp.int32) + (position >= tail_start).astype(jnp.int32)
    ids_total = ids_total + (position >= pad_start).astype(jnp.int32)
    return (ids_total, (position < pad_start).astype(jnp.int32))


def draw_seg_ids(key, part):
    layout = segment_layout(key)
    return layout[0]


def draw_pad_mask(key, part):
    layout = segment_layout(key)
    return layout[1]


def level_of(stream_key, shape, shards, low, high):
    level, own = 1.0, jax.random.fold_in(stream_key, 6)
    for dim, shards_of in shards:
        heights = jnp.exp(jax.random.uniform(jax.random.fold_in(own, dim), (shards_of,), jnp.float32, low / len(shards), high / len(shards)))
        level = level * jnp.repeat(heights, shape[dim] // shards_of).reshape([-1 if axis == dim else 1 for axis in range(len(shape))])
    return level


def normal_values(rng, shape, width, limit, pieces=(), kind=jnp.bfloat16):
    level = level_of(rng, shape, pieces, -0.22, 0.18) if pieces else 1.0
    entries = jax.random.normal(rng, shape, jnp.float32) * width * level
    return jnp.minimum(jnp.maximum(entries, -limit), limit).astype(kind)


def setup_inputs(seed: int = 0) -> dict:
    arg_keys = jax.random.split(jax.random.key(seed), 14)
    layer_in = normal_values(arg_keys[0], (ROWS, SEQ, D), 1.0, 6.0, ((0, 16), (1, 2)))
    seg_ids = draw_seg_ids(jax.random.fold_in(arg_keys[13], 71), 0)
    pad_mask = draw_pad_mask(jax.random.fold_in(arg_keys[13], 71), 0)
    wq = normal_values(arg_keys[3], (D, D), (D // 4) ** -0.5, 0.375, ((1, 2),))
    wk = normal_values(arg_keys[4], (D, D), D ** -0.5, 0.1875, ((1, 2),))
    wv = normal_values(arg_keys[5], (D, D), D ** -0.5, 0.1875, ((1, 2),))
    wo = normal_values(arg_keys[6], (D, D), (D // 64) ** -0.5, 1.5, ((0, 2),))
    wi0 = normal_values(arg_keys[7], (D, FF), D ** -0.5, 0.1875, ((1, 2),))
    wi1 = normal_values(arg_keys[8], (D, FF), D ** -0.5, 0.1875, ((1, 2),))
    wf = normal_values(arg_keys[9], (FF, D), FF ** -0.5, 0.109375, ((0, 2),))
    gain_attn = jnp.clip(1.0 + 0.1 * jax.random.normal(arg_keys[10], (D,), jnp.float32), 0.5, 1.5)
    gain_ffn = jnp.clip(1.0 + 0.1 * jax.random.normal(arg_keys[11], (D,), jnp.float32), 0.5, 1.5)
    out_grad = normal_values(arg_keys[12], (ROWS, SEQ, D), 1.0, 6.0, ((0, 16), (1, 2)))
    return {"layer_in": layer_in, "seg_ids": seg_ids, "pad_mask": pad_mask, "wq": wq, "wk": wk, "wv": wv, "wo": wo, "wi0": wi0, "wi1": wi1, "wf": wf, "gain_attn": gain_attn, "gain_ffn": gain_ffn, "out_grad": out_grad}


EPSILON = 1e-06
HIGHEST = lax.Precision.HIGHEST

@jax.custom_vjp
def low(v):
    return lax.optimization_barrier(v.astype(jnp.bfloat16)).astype(jnp.float32)

@jax.custom_vjp
def low_back(v):
    return v

def low_keep(v):
    return (low(v), None)

def low_pass(kept, grad):
    return (grad,)

def back_keep(v):
    return (v, None)

def back_low(kept, grad):
    return (low(grad),)
low.defvjp(low_keep, low_pass)
low_back.defvjp(back_keep, back_low)

def rms_scale(values, gain):
    return values * lax.rsqrt(lax.optimization_barrier(jnp.mean(values * values, axis=-1, keepdims=True)) + EPSILON) * gain

def allowed_keys(seg_row, mask_row, begin_at, num_rows):
    seg_query = lax.dynamic_slice_in_dim(seg_row, begin_at, num_rows)
    query_pos = begin_at + jnp.arange(num_rows, dtype=jnp.int32)
    key_pos = jnp.arange(seg_row.shape[0], dtype=jnp.int32)
    same_doc = seg_query[:, None] == seg_row[None, :]
    visible = (mask_row[None, :] == 1) | (query_pos[:, None] == key_pos[None, :])
    return same_doc & visible

def attend_block(begin_at, queries, key_heads, value_heads, seg_row, mask_row, block_len):
    query_block = lax.dynamic_slice_in_dim(queries, begin_at, block_len)
    raw = low_back(jnp.einsum('qhd,khd->hqk', query_block, key_heads, precision=HIGHEST))
    allowed = allowed_keys(seg_row, mask_row, begin_at, block_len)
    logits = jnp.where(allowed[None], raw * HD ** (-0.5), -1000000000.0)
    top = lax.optimization_barrier(jnp.max(logits, axis=-1, keepdims=True))
    expo = jnp.exp(logits - top)
    softmax_w = low(expo / lax.optimization_barrier(jnp.sum(expo, axis=-1, keepdims=True)))
    return jnp.einsum('hqk,khd->qhd', softmax_w, value_heads, precision=HIGHEST)

def layer(xf, wq, wk, wv, wo, wi0, wi1, wf, gain_attn, gain_ffn, seg_row, mask_row):
    block_len = min(512, SEQ)
    norm1 = low(rms_scale(xf, gain_attn))
    queries = low_back(low(jnp.dot(norm1, wq, precision=HIGHEST))).reshape(SEQ, H, HD)
    key_heads = low_back(low(jnp.dot(norm1, wk, precision=HIGHEST))).reshape(SEQ, H, HD)
    value_heads = low_back(low(jnp.dot(norm1, wv, precision=HIGHEST))).reshape(SEQ, H, HD)
    block_starts = jnp.arange(SEQ // block_len, dtype=jnp.int32) * block_len
    blocks = lax.map(jax.checkpoint(lambda begin_at: attend_block(begin_at, queries, key_heads, value_heads, seg_row, mask_row, block_len)), block_starts)
    context = low_back(low(blocks.reshape(SEQ, D)))
    branch = low_back(jnp.dot(context, wo, precision=HIGHEST))
    hidden_in = xf + branch
    norm2 = low(rms_scale(hidden_in, gain_ffn))
    gate = low_back(jnp.dot(norm2, wi0, precision=HIGHEST))
    upward = low_back(jnp.dot(norm2, wi1, precision=HIGHEST))
    hidden = low(jax.nn.gelu(gate, approximate=True) * upward)
    return hidden_in + low_back(jnp.dot(hidden, wf, precision=HIGHEST))

def reference(layer_in, seg_ids, pad_mask, wq, wk, wv, wo, wi0, wi1, wf, gain_attn, gain_ffn, out_grad):
    weights = tuple((w.astype(jnp.float32) for w in (wq, wk, wv, wo, wi0, wi1, wf, gain_attn, gain_ffn)))

    def row_step(totals, inputs):
        x_row, seg_row, mask_row, grad_row = inputs

        def forward(xf, *params):
            return layer(xf, *params, seg_row, mask_row)
        result, pull = jax.vjp(forward, x_row.astype(jnp.float32), *weights)
        grads = pull(grad_row.astype(jnp.float32))
        totals = tuple((total + grad for total, grad in zip(totals, grads[1:])))
        return (totals, (result.astype(jnp.bfloat16), grads[0]))
    start_totals = tuple((jnp.zeros(w.shape, jnp.float32) for w in weights))
    totals, (layer_out, d_x) = lax.scan(row_step, start_totals, (layer_in, seg_ids, pad_mask, out_grad))
    return (layer_out, d_x, totals[0], totals[1], totals[2], totals[3], totals[4], totals[5], totals[6], totals[7], totals[8])
```

```python
import functools

import jax
import jax.numpy as jnp
from jax import lax
from jax.experimental import pallas as pl
from jax.experimental.pallas import tpu as pltpu
from jax.sharding import PartitionSpec as P

HD = 64
LANES = 128
EPSILON = 1e-06
BIG = 2.0**30
F32 = jnp.float32
BF16 = jnp.bfloat16
NN = (((1,), (0,)), ((), ()))
NT = (((1,), (1,)), ((), ()))
MIB = 1 << 20


def dot(lhs, rhs, dims=NN):
    return lax.dot_general(lhs, rhs, dims, preferred_element_type=F32)


def call(kernel, name, grid, in_specs, out_specs, out_shape, args, flops, vmem, aliases=None):
    return pl.pallas_call(
        kernel,
        grid=grid,
        in_specs=in_specs,
        out_specs=out_specs,
        out_shape=out_shape,
        input_output_aliases=aliases or {},
        compiler_params=pltpu.CompilerParams(vmem_limit_bytes=vmem * MIB),
        cost_estimate=pl.CostEstimate(
            flops=int(flops),
            bytes_accessed=sum(a.size * a.dtype.itemsize for a in (*args, *jax.tree.leaves(out_shape))),
            transcendentals=0,
        ),
        name=name,
    )(*args)


def whole(array):
    zeros = (0,) * array.ndim
    return pl.BlockSpec(array.shape, lambda *_: zeros)


def shape(dims, dtype):
    return jax.ShapeDtypeStruct(dims, dtype)


SMEM_SPEC = pl.BlockSpec(memory_space=pltpu.SMEM)


def store_transposed(place_ref, values, out_ref, bits):
    turned = jnp.transpose(values)
    count = len(bits)
    rows = turned.shape[0] >> count
    for index in range(1 << count):
        target = 0
        for at, bit in enumerate(bits):
            own = 1 - (place_ref[bit] ^ ((index >> bit) & 1))
            target = target + own * (1 << (count - 1 - at))
        out_ref[pl.ds(pl.multiple_of(target * rows, rows), rows), :] = turned[
            index * rows : (index + 1) * rows
        ]


def project_kernel(bits, place, x_ref, gain_ref, wq_ref, wk_ref, wv_ref, *rest):
    qkv_ref, turned_ref = rest[-2:]
    x = x_ref[...].astype(F32)
    inverse = lax.rsqrt(jnp.mean(x * x, axis=1, keepdims=True) + EPSILON)
    norm = (x * inverse * gain_ref[...]).astype(BF16)
    cols = wq_ref.shape[1]
    for index, weight in enumerate((wq_ref, wk_ref, wv_ref)):
        qkv_ref[:, index * cols : (index + 1) * cols] = dot(norm, weight[...]).astype(BF16)
    store_transposed(place, norm, turned_ref, bits)


def project(place, bits, x, gain, wq, wk, wv, buffer, part, seq_len):
    rows, width = x.shape
    block = min(256, rows)
    steps = rows // block
    cols = wq.shape[1]
    args = [place, x, gain, wq, wk, wv]
    specs = [
        SMEM_SPEC,
        pl.BlockSpec((block, width), lambda i: (i, 0)),
        whole(gain),
        whole(wq),
        whole(wk),
        whole(wv),
    ]
    aliases = {}
    if buffer is not None:
        args.append(buffer)
        specs.append(pl.BlockSpec(memory_space=pl.ANY))
        aliases = {6: 0}
    return call(
        functools.partial(project_kernel, bits),
        "project",
        (steps,),
        specs,
        [
            pl.BlockSpec((block, 3 * cols), lambda i: (part * steps + i, 0)),
            pl.BlockSpec((width, block), lambda i: (0, i)),
        ],
        [shape((seq_len, 3 * cols), BF16), shape((width, rows), BF16)],
        args,
        2.5 * rows * width * 3 * cols,
        16,
        aliases=aliases,
    )


def mask_features(seg, pad):
    lane = jnp.arange(LANES) % HD
    same = seg[:, None] == lane[None, :]
    seg_lane = (lane < 6)[None, :]
    pad_lane = (lane == 6)[None, :]
    query = jnp.where(seg_lane & ~same, -BIG, 0.0) + jnp.where(pad_lane, -BIG, 0.0)
    key = jnp.where(seg_lane & same, 1.0, 0.0)
    key = key + jnp.where(pad_lane & (pad[:, None] == 0), 1.0, 0.0)
    key = key + jnp.where((lane >= 7) & (lane < 10), 1.0, 0.0)[None, :]
    return query.astype(BF16), key.astype(BF16)


def split3(values):
    high = values.astype(BF16)
    rest = values - high.astype(F32)
    middle = rest.astype(BF16)
    return high, middle, (rest - middle.astype(F32)).astype(BF16)


def attend_kernel(
    q_ref, k_ref, v_ref, kd_ref, vd_ref, fq_ref, fk_ref, pad_ref, ctx_ref, qa_ref, qb_ref
):
    block = q_ref.shape[0]
    low = lax.broadcasted_iota(jnp.int32, q_ref.shape, 1) < HD
    low_key = lax.broadcasted_iota(jnp.int32, k_ref.shape, 1) < HD
    row = lax.broadcasted_iota(jnp.int32, (LANES, block), 0)
    upper = row < HD
    inner = row & (HD - 1)
    q = q_ref[...] * BF16(HD**-0.5)
    k = k_ref[...]
    fq = fq_ref[...]
    fk = fk_ref[...]
    v_t = jnp.transpose(v_ref[...])
    upper_v = lax.broadcasted_iota(jnp.int32, v_t.shape, 0) < HD
    one = jnp.ones((), BF16)
    v_own = jnp.transpose(vd_ref[...]).astype(F32)
    product = jnp.transpose(q.astype(F32) * kd_ref[...].astype(F32))
    padded = pad_ref[...] == 0
    outs, log_totals = [], []
    for head in range(2):
        first = head == 0
        q_head = jnp.where(low, q, fq) if first else jnp.where(low, fq, q)
        k_head = jnp.where(low_key, k, fk) if first else jnp.where(low_key, fk, k)
        v_head = jnp.where(upper_v, v_t, one) if first else jnp.where(upper_v, one, v_t)
        mine = upper if first else ~upper
        own = jnp.sum(product[head * HD : head * HD + HD], axis=0, keepdims=True)
        own = jnp.where(padded, own, -1e30)
        scores = dot(k_head, q_head, NT)
        top = jnp.maximum(jnp.max(scores, axis=0, keepdims=True), own)
        expo = jnp.exp(scores - top).astype(BF16)
        both = dot(v_head, expo) + jnp.exp(own - top) * jnp.where(mine, v_own, 1.0)
        total = both[HD : HD + 1] if first else both[0:1]
        outs.append(both / total)
        log_totals.append(split3(-(top + jnp.log(total))))
    ctx_ref[...] = jnp.transpose(jnp.where(upper, outs[0], outs[1])).astype(BF16)
    extra = jnp.zeros((LANES, block), F32)
    for at in range(3):
        piece = jnp.where(upper, log_totals[1][at].astype(F32), log_totals[0][at].astype(F32))
        extra = jnp.where(inner == 7 + at, piece, extra)
    fq = fq + jnp.transpose(extra).astype(BF16)
    qa_ref[...] = jnp.where(low, q, fq)
    qb_ref[...] = jnp.where(low, fq, q)


def attend(qkv, fq, fk, pad, first, pairs):
    seq_len, cols = qkv.shape[0], qkv.shape[1] // 3
    total = cols // LANES
    block = min(1024, seq_len)
    rows = lambda at: pl.BlockSpec((block, LANES), lambda p, i: (i, at * total + first + p))
    full = lambda at: pl.BlockSpec((seq_len, LANES), lambda p, i: (0, at * total + first + p))
    return call(
        attend_kernel,
        "attend",
        (pairs, seq_len // block),
        [
            rows(0),
            full(1),
            full(2),
            rows(1),
            rows(2),
            pl.BlockSpec((block, LANES), lambda p, i: (i, 0)),
            whole(fk),
            pl.BlockSpec((1, block), lambda p, i: (0, i)),
        ],
        [pl.BlockSpec((block, LANES), lambda p, i: (i, p))] * 3,
        [shape((seq_len, pairs * LANES), BF16)] * 3,
        (qkv, qkv, qkv, qkv, qkv, fq, fk, pad.reshape(1, seq_len)),
        4000 * seq_len * seq_len * pairs,
        36,
    )


def attend_back_kernel(
    qa_ref, qb_ref, k_ref, v_ref, fk_ref, pad_ref, ctx_ref, dctx_ref, out_ref
):
    lane = lax.broadcasted_iota(jnp.int32, k_ref.shape, 1)
    low = lane < HD
    inner = lane & (HD - 1)
    k = k_ref[...]
    v = v_ref[...]
    fk = fk_ref[...]
    k_own = k.astype(F32)
    dctx = dctx_ref[...]
    dctx_f = dctx.astype(F32)
    product = dctx_f * ctx_ref[...].astype(F32)
    product_v = dctx_f * v.astype(F32)
    padded = pad_ref[...] == 0
    one = jnp.ones((), BF16)
    zero = jnp.zeros((), BF16)
    dctx_t = jnp.transpose(dctx)
    dq, dk, dv = [], [], []
    for head in range(2):
        mine = low if head == 0 else ~low
        span = slice(head * HD, head * HD + HD)
        q_head = (qa_ref if head == 0 else qb_ref)[...]
        k_head = jnp.where(mine, k, fk)
        v_head = jnp.where(mine, v, one)
        delta = jnp.sum(jnp.where(mine, product, 0.0), axis=1, keepdims=True)
        high, middle, rest = split3(-delta)
        extra = jnp.where(inner == 0, high, jnp.where(inner == 1, middle, jnp.where(inner == 2, rest, zero)))
        weights = jnp.exp(dot(q_head, k_head, NT))
        d_raw = (weights * dot(jnp.where(mine, dctx, extra), v_head, NT)).astype(BF16)
        q_f = q_head.astype(F32)
        lifted = jnp.sum(jnp.where(~mine & (inner >= 7) & (inner < 10), q_f, 0.0), axis=1, keepdims=True)
        own = jnp.sum(jnp.where(mine, q_f * k_own, 0.0), axis=1, keepdims=True) + lifted
        w_own = jnp.where(padded, jnp.exp(jnp.where(padded, own, 0.0)), 0.0)
        d_own = w_own * (jnp.sum(jnp.where(mine, product_v, 0.0), axis=1, keepdims=True) - delta)
        dq.append(dot(d_raw, k) + d_own * k_own)
        dk.append((dot(jnp.transpose(q_head)[span], d_raw), d_own * q_f))
        dv.append((dot(dctx_t[span], weights.astype(BF16)), w_own * dctx_f))
    out_ref[0] = (jnp.where(low, dq[0], dq[1]) * HD**-0.5).astype(BF16)
    for at, parts in ((1, dk), (2, dv)):
        main = jnp.transpose(jnp.concatenate([parts[0][0], parts[1][0]], axis=0))
        out_ref[at] = (main + jnp.where(low, parts[0][1], parts[1][1])).astype(BF16)


def attend_back(qa, qb, qkv, fk, pad, ctx, dctx, first):
    seq_len, cols = qkv.shape[0], qkv.shape[1] // 3
    total = cols // LANES
    pairs = qa.shape[1] // LANES
    own = pl.BlockSpec((seq_len, LANES), lambda p: (0, p))
    at = lambda which: pl.BlockSpec((seq_len, LANES), lambda p: (0, which * total + first + p))
    return call(
        attend_back_kernel,
        "attend_back",
        (pairs,),
        [own, own, at(1), at(2), whole(fk), whole(pad), own, at(0)],
        pl.BlockSpec((3, seq_len, LANES), lambda p: (0, 0, p)),
        shape((3, seq_len, pairs * LANES), BF16),
        (qa, qb, qkv, qkv, fk, pad, ctx, dctx),
        6700 * seq_len * seq_len * pairs,
        40,
    )


def join_kernel(count, x_ref, gain_ref, wo_ref, *refs):
    ctx_refs = refs[:count]
    h1_ref, norm_ref, joined_ref = refs[count:]
    context = jnp.concatenate([ctx[...] for ctx in ctx_refs], axis=1)
    h1 = x_ref[...].astype(F32) + dot(context, wo_ref[...])
    h1_ref[...] = h1
    inverse = lax.rsqrt(jnp.mean(h1 * h1, axis=1, keepdims=True) + EPSILON)
    norm_ref[...] = (h1 * inverse * gain_ref[...]).astype(BF16)
    joined_ref[0] = context


def join(x, gain, wo, contexts):
    rows, width = x.shape
    block = min(256, rows)
    steps = rows // block
    columns = sum(array.shape[1] for array, _ in contexts)
    wide = pl.BlockSpec((block, width), lambda i: (i, 0))
    ctx_specs = [
        pl.BlockSpec((block, array.shape[1]), functools.partial(lambda at, i: (at * steps + i, 0), at))
        for array, at in contexts
    ]
    return call(
        functools.partial(join_kernel, len(contexts)),
        "join",
        (steps,),
        [wide, whole(gain), whole(wo)] + ctx_specs,
        [wide, wide, pl.BlockSpec((1, block, columns), lambda i: (0, i, 0))],
        [shape((rows, width), F32), shape((rows, width), BF16), shape((1, rows, columns), BF16)],
        (x, gain, wo, *[array for array, _ in contexts]),
        2.5 * rows * width * columns,
        16,
    )


def ffn_kernel(
    bits, place, n_ref, g_ref, wi0_ref, wi1_ref, wf_ref,
    deep_ref, out_ref, dnorm_ref, norm_t_ref, grad_t_ref,
):
    norm = n_ref[...]
    grad = g_ref[...]
    store_transposed(place, norm, norm_t_ref, bits[0])
    store_transposed(place, grad, grad_t_ref, bits[1])
    gate = dot(norm, wi0_ref[...])
    up = dot(norm, wi1_ref[...])
    d_hidden = dot(grad, wf_ref[...], NT)
    slope = 0.7978845608028654
    square = gate * gate
    curve = jnp.tanh(slope * gate * (1.0 + 0.044715 * square))
    half = 0.5 * (1.0 + curve)
    active = gate * half
    d_active = half + 0.5 * gate * (1.0 - curve * curve) * (slope + (3.0 * 0.044715 * slope) * square)
    hidden = (active * up).astype(BF16)
    d_gate = (d_hidden * up * d_active).astype(BF16)
    d_up = (d_hidden * active).astype(BF16)
    deep_ref[0] = d_gate
    deep_ref[1] = d_up
    deep_ref[2] = hidden
    dnorm_ref[...] = (dot(d_gate, wi0_ref[...], NT) + dot(d_up, wi1_ref[...], NT)).astype(BF16)
    out_ref[...] = dot(hidden, wf_ref[...]).astype(BF16)


def ffn(place, bits, norm, grad, wi0, wi1, wf):
    rows, width = norm.shape
    units = wi0.shape[1]
    block = min(256, rows)
    wide = pl.BlockSpec((block, width), lambda i: (i, 0))
    tall = pl.BlockSpec((width, block), lambda i: (0, i))
    return call(
        functools.partial(ffn_kernel, bits),
        "ffn",
        (rows // block,),
        [SMEM_SPEC, wide, wide] + [pl.BlockSpec(memory_space=pltpu.VMEM)] * 3,
        [pl.BlockSpec((3, block, units), lambda i: (0, i, 0)), wide, wide, tall, tall],
        [shape((3, rows, units), BF16)]
        + [shape((rows, width), BF16)] * 2
        + [shape((width, rows), BF16)] * 2,
        (place, norm, grad, wi0, wi1, wf),
        15 * rows * width * units,
        36,
    )


def middle_kernel(dn_ref, h1_ref, gain_ref, g_ref, *rest):
    recv_refs, (dh_ref, branch_ref, dgain_ref) = rest[:-3], rest[-3:]
    d_norm = dn_ref[...].astype(F32)
    for recv in recv_refs:
        d_norm = d_norm + recv[...].astype(F32)
    h1 = h1_ref[...]
    inverse = lax.rsqrt(jnp.mean(h1 * h1, axis=1, keepdims=True) + EPSILON)
    normed = h1 * inverse
    scaled = gain_ref[...] * d_norm
    d_h1 = g_ref[...].astype(F32) + inverse * (
        scaled - normed * jnp.mean(scaled * normed, axis=1, keepdims=True)
    )
    dh_ref[...] = d_h1
    branch_ref[...] = d_h1.astype(BF16)

    @pl.when(pl.program_id(0) == 0)
    def _():
        dgain_ref[...] = jnp.zeros_like(dgain_ref)

    dgain_ref[...] += jnp.sum(d_norm * normed, axis=0, keepdims=True)


def middle(d_norm, received, h1, gain, grad):
    rows, width = h1.shape
    block = min(256, rows)
    wide = pl.BlockSpec((block, width), lambda i: (i, 0))
    return call(
        middle_kernel,
        "middle",
        (rows // block,),
        [wide, wide, whole(gain), wide] + [wide] * len(received),
        [wide, wide, pl.BlockSpec((1, width), lambda i: (0, 0))],
        [shape((rows, width), F32), shape((rows, width), BF16), shape((1, width), F32)],
        (d_norm, h1, gain, grad, *received),
        100 * rows * width,
        16,
    )


def dcontext_kernel(bits, place, g_ref, wo_ref, dctx_ref, away_ref, turned_ref):
    grad = g_ref[...]
    d_ctx = dot(grad, wo_ref[...], NT).astype(BF16)
    own = dctx_ref.shape[1]
    dctx_ref[...] = d_ctx[:, :own]
    away_ref[...] = d_ctx[:, own:]
    store_transposed(place, grad, turned_ref, bits)


def dcontext(place, bits, grad, wo, own):
    rows, width = grad.shape
    block = min(256, rows)
    steps = rows // block
    sizes = (own, wo.shape[0] - own)
    return call(
        functools.partial(dcontext_kernel, bits),
        "dcontext",
        (steps,),
        [SMEM_SPEC, pl.BlockSpec((block, width), lambda i: (i, 0)), whole(wo)],
        [pl.BlockSpec((block, size), lambda i: (i, 0)) for size in sizes]
        + [pl.BlockSpec((width, block), lambda i: (0, i))],
        [shape((rows, size), BF16) for size in sizes] + [shape((width, rows), BF16)],
        (place, grad, wo),
        2.5 * rows * width * wo.shape[0],
        16,
    )


def dnorm1(x, grads, weights, part):
    rows, width = x.shape
    block = min(256, rows)
    steps = rows // block
    count = len(grads)

    def kernel(x_ref, *refs):
        grad_refs, w_refs, (dn_ref, dgain_ref) = refs[:count], refs[count:-2], refs[-2:]
        d_norm = None
        for group, g_ref in enumerate(grad_refs):
            size = g_ref.shape[2]
            for which, w_ref in enumerate(w_refs):
                term = dot(g_ref[which], w_ref[:, group * size : (group + 1) * size], NT)
                d_norm = term if d_norm is None else d_norm + term
        dn_ref[...] = d_norm.astype(BF16)
        x = x_ref[...].astype(F32)
        inverse = lax.rsqrt(jnp.mean(x * x, axis=1, keepdims=True) + EPSILON)

        @pl.when(pl.program_id(0) == 0)
        def _():
            dgain_ref[...] = jnp.zeros_like(dgain_ref)

        dgain_ref[...] += jnp.sum(d_norm * (x * inverse), axis=0, keepdims=True)

    wide = pl.BlockSpec((block, width), lambda i: (i, 0))
    return call(
        kernel,
        "dnorm1",
        (steps,),
        [wide]
        + [pl.BlockSpec((3, block, g.shape[2]), lambda i: (0, part * steps + i, 0)) for g in grads]
        + [whole(w) for w in weights],
        [wide, pl.BlockSpec((1, width), lambda i: (0, 0))],
        [shape((rows, width), BF16), shape((1, width), F32)],
        (x, *grads, *weights),
        2.5 * rows * width * 3 * weights[0].shape[1],
        16,
    )


def last_kernel(dn_ref, x_ref, gain_ref, dh_ref, *rest):
    recv_refs, dx_ref = rest[:-1], rest[-1]
    d_norm = dn_ref[...].astype(F32)
    for recv in recv_refs:
        d_norm = d_norm + recv[...].astype(F32)
    x = x_ref[...].astype(F32)
    inverse = lax.rsqrt(jnp.mean(x * x, axis=1, keepdims=True) + EPSILON)
    normed = x * inverse
    scaled = gain_ref[...] * d_norm
    dx_ref[...] = dh_ref[...] + inverse * (
        scaled - normed * jnp.mean(scaled * normed, axis=1, keepdims=True)
    )


def last(d_norm, received, x, gain, d_h1):
    rows, width = x.shape
    block = min(256, rows)
    wide = pl.BlockSpec((block, width), lambda i: (i, 0))
    return call(
        last_kernel,
        "last",
        (rows // block,),
        [wide, wide, whole(gain), wide] + [wide] * len(received),
        wide,
        shape((rows, width), F32),
        (d_norm, x, gain, d_h1, *received),
        100 * rows * width,
        16,
    )


def weight_grads(sides, start, received):
    count = sides[0][0][0].shape[0] // 2
    received = received or []
    lefts = [left for lefts_of, _ in sides for left in lefts_of]
    rights, right_specs, spans = [], [], []
    for lefts_of, rights_of in sides:
        first = spans[-1][1] if spans else 0
        weights, _, columns = rights_of[0][0].shape
        spans.append((first, first + weights))
        for left, (right, at) in zip(lefts_of, rights_of):
            rights.append(right)
            right_specs.append(
                pl.BlockSpec(
                    (1, left.shape[1], columns),
                    functools.partial(
                        lambda f, n, at, w: (jnp.clip(w - f, 0, n - 1), at, 0), first, weights, at
                    ),
                )
            )

    def kernel(*refs):
        left_refs = refs[: len(lefts)]
        right_refs = refs[len(lefts) : len(lefts) + len(rights)]
        recv_refs = refs[len(lefts) + len(rights) : len(refs) - len(sides)]
        out_refs = refs[len(refs) - len(sides) :]
        weight = pl.program_id(0)
        at = 0
        for side, (first, last) in enumerate(spans):

            @pl.when((weight >= first) & (weight < last))
            def _(side=side, at=at):
                total = recv_refs[side][...].astype(F32) if recv_refs else None
                for part in range(at, at + len(sides[side][0])):
                    term = dot(left_refs[part][...], right_refs[part][0])
                    total = term if total is None else total + term
                out_refs[side][...] = total.astype(BF16)

            at += len(sides[side][0])

    out_specs, out_shapes = [], []
    for (_, rights_of), (first, last) in zip(sides, spans):
        columns = rights_of[0][0].shape[2]
        out_specs.append(
            pl.BlockSpec(
                (count, columns),
                functools.partial(lambda f, n, w: (0, jnp.clip(w - f, 0, n - 1)), first, last - first),
            )
        )
        out_shapes.append(shape((count, (last - first) * columns), BF16))
    return call(
        kernel,
        "weight_grads",
        (spans[-1][1],),
        [pl.BlockSpec((count, left.shape[1]), lambda w: (start, 0)) for left in lefts]
        + right_specs
        + (out_specs if received else []),
        out_specs,
        out_shapes,
        (*lefts, *rights, *received),
        2.5 * count * sum(o.shape[1] * l.shape[1] for (ls, _), o in zip(sides, out_shapes) for l in ls),
        24,
    )


def add(left, right):
    return (left.astype(F32) + right.astype(F32)).astype(BF16)


def swap(array, bit):
    size = lax.axis_size("dp")
    return lax.ppermute(array, "dp", [(i, i ^ (1 << bit)) for i in range(size)])


def halve(totals, orders, at):
    halves = [total.shape[0] // 2 for total in totals]
    arrived = [swap(t[:half], order[at]) for t, half, order in zip(totals, halves, orders)]
    return [add(t[half:], a) for t, half, a in zip(totals, halves, arrived)]


def after(value, *others):
    return lax.optimization_barrier((value, *others))[0]


def per_device(
    layer_in, seg_ids, pad_mask, wq, wk, wv, wo, wi0, wi1, wf, gain_attn, gain_ffn, out_grad
):
    dp, mp = lax.axis_size("dp"), lax.axis_size("mp")
    at_dp, at_mp = lax.axis_index("dp"), lax.axis_index("mp")
    bits = tuple(range(dp.bit_length() - 1))
    bits_other = bits[:1] + bits[2:3] + bits[1:2] + bits[3:]
    place = jnp.stack([(at_dp >> bit) & 1 for bit in bits]).astype(jnp.int32)
    seq_len = seg_ids.shape[1]
    x = layer_in[0]
    grad = out_grad[0]
    rows, width = x.shape
    cols = wq.shape[1]
    gain_attn = gain_attn.reshape(1, width)
    gain_ffn = gain_ffn.reshape(1, width)

    def from_shift(array, shift):
        return lax.ppermute(array, "mp", [((d + shift) % mp, d) for d in range(mp)])

    def to_shift(array, shift):
        return lax.ppermute(array, "mp", [(d, (d + shift) % mp) for d in range(mp)])

    own_first = lambda a: jnp.roll(a[0], -at_mp * rows).astype(jnp.int32)
    seg, pad = own_first(seg_ids), own_first(pad_mask)
    fq, fk = mask_features(seg, pad)
    pad = pad.reshape(seq_len, 1)

    wi0, wi1, wf = (pltpu.with_memory_space_constraint(w, pltpu.VMEM) for w in (wi0, wi1, wf))

    x_parts = [x] + [from_shift(x, shift) for shift in range(1, mp)]
    qkv = None
    norm1_t = []
    for part in range(mp):
        qkv, turned = project(
            place, bits, x_parts[part], gain_attn, wq, wk, wv, qkv, part, seq_len
        )
        norm1_t.append(turned)
    piece = wo.shape[0] // dp
    wo_piece = lax.dynamic_slice_in_dim(after(wo, x_parts[-1]), at_dp * piece, piece, 0)
    wo_all = jnp.concatenate(
        [wo]
        + [lax.all_gather(from_shift(wo_piece, shift), "dp", axis=0, tiled=True) for shift in range(1, mp)]
    )
    total_pairs = cols // LANES
    group = max(1, total_pairs // 2)
    groups = [(first, group) for first in range(0, total_pairs, group)]

    saved, near, far = [], [], []
    tail = x_parts[-1]
    for first, pairs in groups:
        ctx, qa, qb = attend(qkv, fq, fk, pad, first, pairs)
        saved.append((qa, qb, ctx))
    g_parts = [grad] + [from_shift(after(grad, tail), shift) for shift in range(1, mp)]
    for shift in range(1, mp):
        for _, _, ctx in saved:
            cut = (mp - shift) * rows
            near.append(from_shift(ctx[cut : cut + rows], shift))
            rest = jnp.concatenate([ctx[cut + rows :], ctx[:cut]])
            far.append(from_shift(rest, shift))

    deep, norm2_t, grad_t, joined, h1, d_norm2, ffn_out = ([None] * mp for _ in range(7))
    ffn_received, dn_received = [], []
    for part in range(mp):
        contexts = [(ctx, part) for _, _, ctx in saved]
        contexts += [(array, part - 1) for array in far] if part else [(array, 0) for array in near]
        source = x_parts[part]
        if part:
            source = after(source, d_norm2[part - 1])
        h1[part], norm2, joined[part] = join(source, gain_ffn, wo_all, contexts)
        deep[part], ffn_out[part], d_norm2[part], norm2_t[part], grad_t[part] = ffn(
            place, (bits, bits_other), norm2, g_parts[part], wi0, wi1, wf
        )
        if part:
            dn_received.append(to_shift(d_norm2[part], part))
            ffn_received.append(to_shift(ffn_out[part], part))

    units = wi0.shape[1]
    cuts = [(0, 2)] if units % LANES == 0 else [(0, 1), (1, 2)]
    ffn_sides = [(norm2_t, [(array[a:b], 0) for array in deep]) for a, b in cuts]
    ffn_sides.append((grad_t, [(array[2:], 0) for array in deep]))
    ffn_orders = [bits] * len(cuts) + [bits_other]
    sent = weight_grads(ffn_sides, 0, None)
    arrived = [swap(array, order[0]) for array, order in zip(sent, ffn_orders)]
    ffn_totals = weight_grads(ffn_sides, 1, arrived)

    d_norm2_own = after(d_norm2[0], *ffn_totals)
    d_h1, branch, dgain_ffn = middle(d_norm2_own, dn_received, h1[0], gain_ffn, grad)
    d_ctx, away, branch_t = dcontext(place, bits, branch, wo_all, cols)
    d_ctx = jnp.concatenate(
        [d_ctx]
        + [
            from_shift(away[:, (mp - shift - 1) * cols : (mp - shift) * cols], shift)
            for shift in range(1, mp)
        ]
    )
    ffn_totals = halve(ffn_totals, ffn_orders, 1)

    layer_out = h1[0] + ffn_out[0].astype(F32)
    for received in ffn_received:
        layer_out = layer_out + received.astype(F32)
    layer_out = layer_out.astype(BF16)

    grads, totals = [], []
    for index, ((first, _), (qa, qb, ctx)) in enumerate(zip(groups, saved)):
        if index:
            qa = after(qa, *totals[-1])
        got = attend_back(qa, qb, qkv, fk, pad, ctx, d_ctx, first)
        grads.append(got)
        sides = [(norm1_t, [(got, part) for part in range(mp)])]
        if index == 0:
            sides.append(([branch_t], [(joined[0], 0)]))
        sent = weight_grads(sides, 0, None)
        arrived = [swap(array, bits[0]) for array in sent]
        if index == len(groups) - 1:
            dn_parts = [
                dnorm1(x_parts[part], grads, (wq, wk, wv), part) for part in list(range(1, mp)) + [0]
            ]
        totals.append(weight_grads(sides, 1, arrived))
    dn1_received = [to_shift(dn_parts[part - 1][0], part) for part in range(1, mp)]

    dgains = jnp.concatenate([sum(p[1] for p in dn_parts), dgain_ffn], axis=0)
    dgains = sum([dgains] + [from_shift(dgains, shift) for shift in range(1, mp)])
    for bit in bits:
        dgains = dgains + swap(dgains, bit)

    for at in range(2, len(bits)):
        ffn_totals = halve(ffn_totals, ffn_orders, at)
    d_wi, d_wf = jnp.concatenate(ffn_totals[:-1], axis=1), ffn_totals[-1]
    for at in range(1, len(bits)):
        totals = [halve(total, [bits] * len(total), at) for total in totals]
    wo_grad = totals[0][1]
    d_wo = sum(
        [wo_grad[:, :cols].astype(F32)]
        + [
            from_shift(wo_grad[:, (mp - shift) * cols : (mp - shift + 1) * cols], shift).astype(F32)
            for shift in range(1, mp)
        ]
    )
    pieces = [total[0].reshape(-1, 3, group * LANES) for total in totals]
    d_wq, d_wk, d_wv = (
        jnp.concatenate([piece[:, which] for piece in pieces], axis=1).astype(F32) for which in range(3)
    )
    d_x = last(dn_parts[-1][0], dn1_received, x, gain_attn, d_h1)
    return (
        layer_out[None],
        d_x[None],
        d_wq,
        d_wk,
        d_wv,
        d_wo.T,
        d_wi[:, :units].astype(F32),
        d_wi[:, units:].astype(F32),
        d_wf.T.astype(F32),
        dgains[0],
        dgains[1],
    )


def solution(mesh):
    return jax.shard_map(
        per_device,
        mesh=mesh,
        in_specs=(
            P("dp", "mp", None),
            P("dp", None),
            P("dp", None),
            P(None, "mp"),
            P(None, "mp"),
            P(None, "mp"),
            P("mp", None),
            P(None, "mp"),
            P(None, "mp"),
            P("mp", None),
            P(),
            P(),
            P("dp", "mp", None),
        ),
        out_specs=(
            P("dp", "mp", None),
            P("dp", "mp", None),
            P("dp", "mp"),
            P("dp", "mp"),
            P("dp", "mp"),
            P("mp", "dp"),
            P("dp", "mp"),
            P("dp", "mp"),
            P("mp", "dp"),
            P(),
            P(),
        ),
        check_vma=False,
    )
```

```python
import functools

import jax
import jax.numpy as jnp
from jax import lax
from jax.experimental import pallas as pl
from jax.experimental.pallas import tpu as pltpu
from jax.sharding import PartitionSpec as P

HD = 64
LANES = 128
EPSILON = 1e-06
BIG = 2.0**30
F32 = jnp.float32
BF16 = jnp.bfloat16
NN = (((1,), (0,)), ((), ()))
NT = (((1,), (1,)), ((), ()))
MIB = 1 << 20


def dot(lhs, rhs, dims=NN):
    return lax.dot_general(lhs, rhs, dims, preferred_element_type=F32)


class Turn:
    def __init__(self):
        self.token = jnp.zeros((1,), jnp.int32)

    def join(self, *arrays):
        self.token, *arrays = lax.optimization_barrier((self.token, *arrays))
        return arrays


def call(turn, kernel, name, grid, in_specs, out_specs, out_shape, args, flops, vmem, scratch=(), stay=False):
    token_at = len(args) + len(out_shape)

    if stay:
        args = [
            pltpu.with_memory_space_constraint(a, pltpu.HBM) if a.size * a.dtype.itemsize > MIB // 4 else a
            for a in args
        ]

    def with_token(token_ref, *refs):
        @pl.when(functools.reduce(lambda a, b: a & b, [pl.program_id(d) == 0 for d in range(len(grid))]))
        def _():
            refs[token_at][0] = 0

        kernel(*refs[:token_at], *refs[token_at + 1 :])

    *outs, turn.token = pl.pallas_call(
        with_token,
        grid=grid,
        in_specs=[pl.BlockSpec(memory_space=pl.ANY), *in_specs],
        out_specs=[*out_specs, pl.BlockSpec(memory_space=pltpu.SMEM)],
        out_shape=[*out_shape, shape((1,), jnp.int32)],
        scratch_shapes=list(scratch),
        compiler_params=pltpu.CompilerParams(vmem_limit_bytes=vmem * MIB),
        cost_estimate=pl.CostEstimate(
            flops=int(0.1 * flops),
            bytes_accessed=int(0.1 * sum(a.size * a.dtype.itemsize for a in (*args, *out_shape))),
            transcendentals=0,
        ),
        name=name,
    )(turn.token, *args)
    return outs


def whole(array):
    zeros = (0,) * array.ndim
    return pl.BlockSpec(array.shape, lambda *_: zeros)


def shape(dims, dtype):
    return jax.ShapeDtypeStruct(dims, dtype)


SMEM_SPEC = pl.BlockSpec(memory_space=pltpu.SMEM)


def store_transposed(place_ref, values, out_ref, bits):
    turned = jnp.transpose(values)
    count = len(bits)
    rows = turned.shape[0] >> count
    for index in range(1 << count):
        target = 0
        for at, bit in enumerate(bits):
            own = 1 - (place_ref[bit] ^ ((index >> bit) & 1))
            target = target + own * (1 << (count - 1 - at))
        out_ref[pl.ds(pl.multiple_of(target * rows, rows), rows), :] = turned[
            index * rows : (index + 1) * rows
        ]


def project_kernel(bits, place, x_ref, gain_ref, wq_ref, wk_ref, wv_ref, qkv_ref, turned_ref):
    x = x_ref[...].astype(F32)
    inverse = lax.rsqrt(jnp.mean(x * x, axis=1, keepdims=True) + EPSILON)
    norm = (x * inverse * gain_ref[...]).astype(BF16)
    cols = wq_ref.shape[1]
    for index, weight in enumerate((wq_ref, wk_ref, wv_ref)):
        qkv_ref[:, index * cols : (index + 1) * cols] = dot(norm, weight[...]).astype(BF16)
    store_transposed(place, norm, turned_ref, bits)


def project(turn, place, bits, x, gain, wq, wk, wv):
    rows, width = x.shape
    block = min(256, rows)
    cols = wq.shape[1]
    return call(
        turn,
        functools.partial(project_kernel, bits),
        "project",
        (rows // block,),
        [
            SMEM_SPEC,
            pl.BlockSpec((block, width), lambda i: (i, 0)),
            whole(gain),
            whole(wq),
            whole(wk),
            whole(wv),
        ],
        [
            pl.BlockSpec((block, 3 * cols), lambda i: (i, 0)),
            pl.BlockSpec((width, block), lambda i: (0, i)),
        ],
        [shape((rows, 3 * cols), BF16), shape((width, rows), BF16)],
        (place, x, gain, wq, wk, wv),
        2.5 * rows * width * 3 * cols,
        20,
    )


def mask_features(seg, pad):
    lane = jnp.arange(LANES) % HD
    same = seg[:, None] == lane[None, :]
    seg_lane = (lane < 6)[None, :]
    pad_lane = (lane == 6)[None, :]
    query = jnp.where(seg_lane & ~same, -BIG, 0.0) + jnp.where(pad_lane, -BIG, 0.0)
    key = jnp.where(seg_lane & same, 1.0, 0.0)
    key = key + jnp.where(pad_lane & (pad[:, None] == 0), 1.0, 0.0)
    key = key + jnp.where((lane >= 7) & (lane < 10), 1.0, 0.0)[None, :]
    return query.astype(BF16), key.astype(BF16)


def split3(values):
    high = values.astype(BF16)
    rest = values - high.astype(F32)
    middle = rest.astype(BF16)
    return high, middle, (rest - middle.astype(F32)).astype(BF16)


def rows_of(refs):
    return jnp.concatenate([ref[...] for ref in refs], axis=0)


def attend_kernel(parts, *refs):
    q_refs, k_refs, v_refs = refs[:parts], refs[parts : 2 * parts], refs[2 * parts : 3 * parts]
    fq_ref, fk_ref, pad_ref = refs[3 * parts : 3 * parts + 3]
    ctx_refs, (qa_ref, qb_ref) = refs[3 * parts + 3 : -2], refs[-2:]
    q = rows_of(q_refs) * BF16(HD**-0.5)
    k = rows_of(k_refs)
    v = rows_of(v_refs)
    block = q.shape[0]
    low = lax.broadcasted_iota(jnp.int32, q.shape, 1) < HD
    row = lax.broadcasted_iota(jnp.int32, (LANES, block), 0)
    upper = row < HD
    inner = row & (HD - 1)
    fq = fq_ref[...]
    fk = fk_ref[...]
    v_t = jnp.transpose(v)
    one = jnp.ones((), BF16)
    v_own = v_t.astype(F32)
    product = jnp.transpose(q.astype(F32) * k.astype(F32))
    padded = pad_ref[...] == 0
    outs, log_totals = [], []
    for head in range(2):
        first = head == 0
        q_head = jnp.where(low, q, fq) if first else jnp.where(low, fq, q)
        k_head = jnp.where(low, k, fk) if first else jnp.where(low, fk, k)
        v_head = jnp.where(upper, v_t, one) if first else jnp.where(upper, one, v_t)
        mine = upper if first else ~upper
        own = jnp.sum(product[head * HD : head * HD + HD], axis=0, keepdims=True)
        own = jnp.where(padded, own, -1e30)
        scores = dot(k_head, q_head, NT)
        top = jnp.maximum(jnp.max(scores, axis=0, keepdims=True), own)
        expo = jnp.exp(scores - top).astype(BF16)
        both = dot(v_head, expo) + jnp.exp(own - top) * jnp.where(mine, v_own, 1.0)
        total = both[HD : HD + 1] if first else both[0:1]
        outs.append(both / total)
        log_totals.append(split3(-(top + jnp.log(total))))
    context = jnp.transpose(jnp.where(upper, outs[0], outs[1])).astype(BF16)
    rows = block // parts
    for part, ctx_ref in enumerate(ctx_refs):
        ctx_ref[...] = context[part * rows : (part + 1) * rows]
    extra = jnp.zeros((LANES, block), F32)
    for at in range(3):
        piece = jnp.where(upper, log_totals[1][at].astype(F32), log_totals[0][at].astype(F32))
        extra = jnp.where(inner == 7 + at, piece, extra)
    fq = fq + jnp.transpose(extra).astype(BF16)
    qa_ref[...] = jnp.where(low, q, fq)
    qb_ref[...] = jnp.where(low, fq, q)


def attend(turn, qkv, fq, fk, pad):
    parts = len(qkv)
    rows, cols = qkv[0].shape[0], qkv[0].shape[1] // 3
    seq_len = parts * rows
    pairs = cols // LANES
    at = lambda which: [pl.BlockSpec((rows, LANES), lambda p: (0, which * pairs + p))] * parts
    tall = pl.BlockSpec((seq_len, LANES), lambda p: (0, p))
    part = pl.BlockSpec((rows, LANES), lambda p: (0, p))
    *ctx, qa, qb = call(
        turn,
        functools.partial(attend_kernel, parts),
        "attend",
        (pairs,),
        at(0) + at(1) + at(2) + [whole(fq), whole(fk), whole(pad)],
        [part] * parts + [tall] * 2,
        [shape((rows, pairs * LANES), BF16)] * parts + [shape((seq_len, pairs * LANES), BF16)] * 2,
        (*qkv, *qkv, *qkv, fq, fk, pad),
        4000 * seq_len * seq_len * pairs,
        40,
        stay=True,
    )
    return ctx, qa, qb


def attend_back_kernel(parts, qa_ref, qb_ref, fk_ref, pad_ref, *refs):
    *refs, out_ref = refs
    k, v, ctx, dctx = (rows_of(refs[at * parts : (at + 1) * parts]) for at in range(4))
    lane = lax.broadcasted_iota(jnp.int32, k.shape, 1)
    low = lane < HD
    inner = lane & (HD - 1)
    fk = fk_ref[...]
    k_own = k.astype(F32)
    dctx_f = dctx.astype(F32)
    product = dctx_f * ctx.astype(F32)
    product_v = dctx_f * v.astype(F32)
    padded = pad_ref[...] == 0
    one = jnp.ones((), BF16)
    zero = jnp.zeros((), BF16)
    dctx_t = jnp.transpose(dctx)
    dq, dk, dv = [], [], []
    for head in range(2):
        mine = low if head == 0 else ~low
        span = slice(head * HD, head * HD + HD)
        q_head = (qa_ref if head == 0 else qb_ref)[...]
        k_head = jnp.where(mine, k, fk)
        v_head = jnp.where(mine, v, one)
        delta = jnp.sum(jnp.where(mine, product, 0.0), axis=1, keepdims=True)
        high, middle, rest = split3(-delta)
        extra = jnp.where(inner == 0, high, jnp.where(inner == 1, middle, jnp.where(inner == 2, rest, zero)))
        weights = jnp.exp(dot(q_head, k_head, NT))
        d_raw = (weights * dot(jnp.where(mine, dctx, extra), v_head, NT)).astype(BF16)
        q_f = q_head.astype(F32)
        lifted = jnp.sum(jnp.where(~mine & (inner >= 7) & (inner < 10), q_f, 0.0), axis=1, keepdims=True)
        own = jnp.sum(jnp.where(mine, q_f * k_own, 0.0), axis=1, keepdims=True) + lifted
        w_own = jnp.where(padded, jnp.exp(jnp.where(padded, own, 0.0)), 0.0)
        d_own = w_own * (jnp.sum(jnp.where(mine, product_v, 0.0), axis=1, keepdims=True) - delta)
        dq.append(dot(d_raw, k) + d_own * k_own)
        dk.append((dot(jnp.transpose(q_head)[span], d_raw), d_own * q_f))
        dv.append((dot(dctx_t[span], weights.astype(BF16)), w_own * dctx_f))
    out_ref[0] = (jnp.where(low, dq[0], dq[1]) * HD**-0.5).astype(BF16)
    for at, parts in ((1, dk), (2, dv)):
        main = jnp.transpose(jnp.concatenate([parts[0][0], parts[1][0]], axis=0))
        out_ref[at] = (main + jnp.where(low, parts[0][1], parts[1][1])).astype(BF16)


def attend_back(turn, qa, qb, qkv, fk, pad, ctx, dctx, first, pairs):
    parts = len(qkv)
    rows, cols = qkv[0].shape[0], qkv[0].shape[1] // 3
    seq_len = parts * rows
    total = cols // LANES
    tall = pl.BlockSpec((seq_len, LANES), lambda p: (0, first + p))
    part = [pl.BlockSpec((rows, LANES), lambda p: (0, first + p))] * parts
    at = lambda which: [pl.BlockSpec((rows, LANES), lambda p: (0, which * total + first + p))] * parts
    return call(
        turn,
        functools.partial(attend_back_kernel, parts),
        "attend_back",
        (pairs,),
        [tall, tall, whole(fk), whole(pad)] + at(1) + at(2) + part + at(0),
        [pl.BlockSpec((3, seq_len, LANES), lambda p: (0, 0, p))],
        [shape((3, seq_len, pairs * LANES), BF16)],
        (qa, qb, fk, pad, *qkv, *qkv, *ctx, *dctx),
        6700 * seq_len * seq_len * pairs,
        44,
        stay=True,
    )[0]


def feed_kernel(bits, counts, place, x_ref, gain_ref, g_ref, *refs):
    heads, groups, own = counts
    wo_refs, refs = refs[:heads], refs[heads:]
    ctx_refs, refs = refs[:groups], refs[groups:]
    sources, refs = refs[:3], refs[3:]
    deep_ref, out_ref, dnorm_ref, norm_t_ref, grad_t_ref = refs[:5]
    wi0_ref, wi1_ref, wf_ref, arrived = refs[-4:]
    first = pl.program_id(0) == 0
    copies = [
        pltpu.make_async_copy(source, target, arrived.at[at])
        for at, (source, target) in enumerate(zip(sources, (wi0_ref, wi1_ref, wf_ref)))
    ]

    @pl.when(first)
    def _():
        for copy in copies:
            copy.start()

    context = jnp.concatenate([ctx[...] for ctx in ctx_refs], axis=1)
    h1 = x_ref[...].astype(F32)
    at = 0
    for wo_ref in wo_refs:
        h1 = h1 + dot(context[:, at : at + wo_ref.shape[0]], wo_ref[...])
        at += wo_ref.shape[0]
    if own:
        h1_ref, joined_ref = refs[5:7]
        h1_ref[...] = h1
        for at in range(joined_ref.shape[0]):
            joined_ref[at] = context[:, at * joined_ref.shape[2] : (at + 1) * joined_ref.shape[2]]
    inverse = lax.rsqrt(jnp.mean(h1 * h1, axis=1, keepdims=True) + EPSILON)
    norm = (h1 * inverse * gain_ref[...]).astype(BF16)
    grad = g_ref[...]
    store_transposed(place, norm, norm_t_ref, bits[0])
    store_transposed(place, grad, grad_t_ref, bits[1])

    pl.when(first)(copies[0].wait)
    gate = dot(norm, wi0_ref[...])
    pl.when(first)(copies[1].wait)
    up = dot(norm, wi1_ref[...])
    pl.when(first)(copies[2].wait)
    d_hidden = dot(grad, wf_ref[...], NT)
    slope = 0.7978845608028654
    square = gate * gate
    curve = jnp.tanh(slope * gate * (1.0 + 0.044715 * square))
    half = 0.5 * (1.0 + curve)
    active = gate * half
    d_active = half + 0.5 * gate * (1.0 - curve * curve) * (slope + (3.0 * 0.044715 * slope) * square)
    hidden = (active * up).astype(BF16)
    d_gate = (d_hidden * up * d_active).astype(BF16)
    d_up = (d_hidden * active).astype(BF16)
    deep_ref[0] = d_gate
    deep_ref[1] = d_up
    deep_ref[2] = hidden
    dnorm_ref[...] = (dot(d_gate, wi0_ref[...], NT) + dot(d_up, wi1_ref[...], NT)).astype(BF16)
    out_ref[...] = dot(hidden, wf_ref[...]).astype(BF16)


def feed(turn, place, bits, x, gain, grad, wo_parts, contexts, weights, own):
    rows, width = x.shape
    units = weights[0].shape[1]
    block = min(256, rows)
    steps = rows // block
    columns = sum(array.shape[1] for array, _ in contexts)
    wide = pl.BlockSpec((block, width), lambda i: (i, 0))
    tall = pl.BlockSpec((width, block), lambda i: (0, i))
    ctx_specs = [
        pl.BlockSpec((block, array.shape[1]), functools.partial(lambda at, i: (at * steps + i, 0), at))
        for array, at in contexts
    ]
    out_specs = [pl.BlockSpec((3, block, units), lambda i: (0, i, 0)), wide, wide, tall, tall]
    out_shapes = (
        [shape((3, rows, units), BF16)]
        + [shape((rows, width), BF16)] * 2
        + [shape((width, rows), BF16)] * 2
    )
    if own:
        out_specs += [wide, pl.BlockSpec((columns // own, block, own), lambda i: (0, i, 0))]
        out_shapes += [shape((rows, width), F32), shape((columns // own, rows, own), BF16)]
    kernel = functools.partial(feed_kernel, bits, (len(wo_parts), len(contexts), own))
    return call(
        turn,
        kernel,
        "feed",
        (steps,),
        [SMEM_SPEC, wide, whole(gain), wide]
        + [whole(w) for w in wo_parts]
        + ctx_specs
        + [pl.BlockSpec(memory_space=pl.ANY)] * 3,
        out_specs,
        out_shapes,
        (place, x, gain, grad, *wo_parts, *[array for array, _ in contexts], *weights),
        rows * width * (15 * units + 2.5 * columns),
        48,
        scratch=[pltpu.VMEM(w.shape, BF16) for w in weights] + [pltpu.SemaphoreType.DMA((3,))],
        stay=True,
    )


def middle_kernel(bits, heads, place, dn_ref, h1_ref, gain_ref, g_ref, *refs):
    wo_refs, refs = refs[:heads], refs[heads:]
    recv_refs, (dh_ref, dgain_ref, turned_ref, *dctx_refs) = refs[: -3 - heads], refs[-3 - heads :]
    d_norm = dn_ref[...].astype(F32)
    for recv in recv_refs:
        d_norm = d_norm + recv[...].astype(F32)
    h1 = h1_ref[...]
    inverse = lax.rsqrt(jnp.mean(h1 * h1, axis=1, keepdims=True) + EPSILON)
    normed = h1 * inverse
    scaled = gain_ref[...] * d_norm
    d_h1 = g_ref[...].astype(F32) + inverse * (
        scaled - normed * jnp.mean(scaled * normed, axis=1, keepdims=True)
    )
    dh_ref[...] = d_h1
    branch = d_h1.astype(BF16)
    for wo_ref, dctx_ref in zip(wo_refs, dctx_refs):
        dctx_ref[...] = dot(branch, wo_ref[...], NT).astype(BF16)
    store_transposed(place, branch, turned_ref, bits)

    @pl.when(pl.program_id(0) == 0)
    def _():
        dgain_ref[...] = jnp.zeros_like(dgain_ref)

    dgain_ref[...] += jnp.sum(d_norm * normed, axis=0, keepdims=True)


def middle(turn, place, bits, d_norm, received, h1, gain, grad, wo_parts):
    rows, width = h1.shape
    block = min(256, rows)
    heads = len(wo_parts)
    wide = pl.BlockSpec((block, width), lambda i: (i, 0))
    return call(
        turn,
        functools.partial(middle_kernel, bits, heads),
        "middle",
        (rows // block,),
        [SMEM_SPEC, wide, wide, whole(gain), wide] + [whole(w) for w in wo_parts] + [wide] * len(received),
        [wide, pl.BlockSpec((1, width), lambda i: (0, 0)), pl.BlockSpec((width, block), lambda i: (0, i))]
        + [pl.BlockSpec((block, w.shape[0]), lambda i: (i, 0)) for w in wo_parts],
        [shape((rows, width), F32), shape((1, width), F32), shape((width, rows), BF16)]
        + [shape((rows, w.shape[0]), BF16) for w in wo_parts],
        (place, d_norm, h1, gain, grad, *wo_parts, *received),
        2.5 * rows * width * sum(w.shape[0] for w in wo_parts),
        20,
    )


def dnorm1(turn, x, grads, weights, part):
    rows, width = x.shape
    block = min(256, rows)
    steps = rows // block
    count = len(grads)

    def kernel(x_ref, *refs):
        grad_refs, w_refs, (dn_ref, dgain_ref) = refs[:count], refs[count:-2], refs[-2:]
        d_norm = None
        for group, g_ref in enumerate(grad_refs):
            size = g_ref.shape[2]
            for which, w_ref in enumerate(w_refs):
                term = dot(g_ref[which], w_ref[:, group * size : (group + 1) * size], NT)
                d_norm = term if d_norm is None else d_norm + term
        dn_ref[...] = d_norm.astype(BF16)
        x = x_ref[...].astype(F32)
        inverse = lax.rsqrt(jnp.mean(x * x, axis=1, keepdims=True) + EPSILON)

        @pl.when(pl.program_id(0) == 0)
        def _():
            dgain_ref[...] = jnp.zeros_like(dgain_ref)

        dgain_ref[...] += jnp.sum(d_norm * (x * inverse), axis=0, keepdims=True)

    wide = pl.BlockSpec((block, width), lambda i: (i, 0))
    return call(
        turn,
        kernel,
        "dnorm1",
        (steps,),
        [wide]
        + [pl.BlockSpec((3, block, g.shape[2]), lambda i: (0, part * steps + i, 0)) for g in grads]
        + [whole(w) for w in weights],
        [wide, pl.BlockSpec((1, width), lambda i: (0, 0))],
        [shape((rows, width), BF16), shape((1, width), F32)],
        (x, *grads, *weights),
        2.5 * rows * width * 3 * weights[0].shape[1],
        20,
    )


def last_kernel(dn_ref, x_ref, gain_ref, dh_ref, *rest):
    recv_refs, dx_ref = rest[:-1], rest[-1]
    d_norm = dn_ref[...].astype(F32)
    for recv in recv_refs:
        d_norm = d_norm + recv[...].astype(F32)
    x = x_ref[...].astype(F32)
    inverse = lax.rsqrt(jnp.mean(x * x, axis=1, keepdims=True) + EPSILON)
    normed = x * inverse
    scaled = gain_ref[...] * d_norm
    dx_ref[...] = dh_ref[...] + inverse * (
        scaled - normed * jnp.mean(scaled * normed, axis=1, keepdims=True)
    )


def last(turn, d_norm, received, x, gain, d_h1):
    rows, width = x.shape
    block = min(256, rows)
    wide = pl.BlockSpec((block, width), lambda i: (i, 0))
    return call(
        turn,
        last_kernel,
        "last",
        (rows // block,),
        [wide, wide, whole(gain), wide] + [wide] * len(received),
        [wide],
        [shape((rows, width), F32)],
        (d_norm, x, gain, d_h1, *received),
        100 * rows * width,
        20,
    )[0]


def weight_grads(turn, sides, start, received, joint=False):
    count = sides[0][0][0].shape[0] // 2
    received = received or []
    cuts = 2 if received else 1
    lefts = [left for side in sides for left in side[0]]
    rights, right_specs, spans = [], [], []
    for lefts_of, rights_of, lowest, weights in sides:
        first = spans[-1][1] if spans else 0
        columns = rights_of[0][0].shape[2]
        spans.append((first, first + weights))
        for left, (right, at) in zip(lefts_of, rights_of):
            rights.append(right)
            right_specs.append(
                pl.BlockSpec(
                    (1, left.shape[1], columns),
                    functools.partial(
                        lambda f, n, low, at, w: (low + jnp.clip(w - f, 0, n - 1), at, 0),
                        first, weights, lowest, at,
                    ),
                )
            )

    wholes = [(0, spans[-1][1])] if joint else spans
    outputs = len(wholes)

    def kernel(*refs):
        left_refs = refs[: len(lefts)]
        right_refs = refs[len(lefts) : len(lefts) + len(rights)]
        recv_refs = refs[len(lefts) + len(rights) : len(refs) - cuts * outputs]
        out_refs = refs[len(refs) - cuts * outputs :]
        weight = pl.program_id(0)
        at = 0
        for side, (first, last) in enumerate(spans):

            @pl.when((weight >= first) & (weight < last))
            def _(side=side, at=at):
                out = 0 if joint else side
                total = recv_refs[out][...].astype(F32) if recv_refs else None
                for part in range(at, at + len(sides[side][0])):
                    term = dot(left_refs[part][...], right_refs[part][0])
                    total = term if total is None else total + term
                rows = count // cuts
                for cut in range(cuts):
                    out_refs[out * cuts + cut][...] = total[cut * rows : (cut + 1) * rows].astype(BF16)

            at += len(sides[side][0])

    widths = [side[1][0][0].shape[2] for side in sides][:outputs]

    def specs(rows):
        return [
            pl.BlockSpec(
                (rows, columns),
                functools.partial(lambda f, n, w: (0, jnp.clip(w - f, 0, n - 1)), first, last - first),
            )
            for columns, (first, last) in zip(widths, wholes)
        ]

    out_specs, out_shapes = [], []
    for spec, columns, (first, last) in zip(specs(count // cuts), widths, wholes):
        out_specs += [spec] * cuts
        out_shapes += [shape((count // cuts, (last - first) * columns), BF16)] * cuts
    outs = call(
        turn,
        kernel,
        "weight_grads",
        (spans[-1][1],),
        [pl.BlockSpec((count, left.shape[1]), lambda w: (start, 0)) for left in lefts]
        + right_specs
        + (specs(count) if received else []),
        out_specs,
        out_shapes,
        (*lefts, *rights, *received),
        2.5 * count * sum(side[3] * side[1][0][0].shape[2] * l.shape[1] for side in sides for l in side[0]),
        28,
    )
    return [tuple(outs[at : at + 2]) for at in range(0, len(outs), 2)] if received else outs


def add(left, right):
    return (left.astype(F32) + right.astype(F32)).astype(BF16)


def swap(array, bit):
    size = lax.axis_size("dp")
    return lax.ppermute(array, "dp", [(i, i ^ (1 << bit)) for i in range(size)])


def halve(turn, totals, arrived):
    outs = []
    arrived = turn.join(*arrived)
    for (_, kept), came in zip(totals, arrived):
        cut = kept.shape[0] // 2
        outs.append((add(kept[:cut], came[:cut]), add(kept[cut:], came[cut:])))
    flat = turn.join(*[part for pair in outs for part in pair])
    return list(zip(flat[::2], flat[1::2]))


def finish(totals, arrived):
    return [kept.astype(F32) + came.astype(F32) for (_, kept), came in zip(totals, arrived)]


def exchange(totals, orders, at):
    return [swap(send, order[at]) for (send, _), order in zip(totals, orders)]


def per_device(
    layer_in, seg_ids, pad_mask, wq, wk, wv, wo, wi0, wi1, wf, gain_attn, gain_ffn, out_grad
):
    dp, mp = lax.axis_size("dp"), lax.axis_size("mp")
    at_dp, at_mp = lax.axis_index("dp"), lax.axis_index("mp")
    bits = tuple(range(dp.bit_length() - 1))
    bits_other = bits[:1] + bits[2:3] + bits[1:2] + bits[3:]
    place = jnp.stack([(at_dp >> bit) & 1 for bit in bits]).astype(jnp.int32)
    seq_len = seg_ids.shape[1]
    x = layer_in[0]
    grad = out_grad[0]
    rows, width = x.shape
    cols = wq.shape[1]
    gain_attn = gain_attn.reshape(1, width)
    gain_ffn = gain_ffn.reshape(1, width)

    def from_shift(array, shift):
        return lax.ppermute(array, "mp", [((d + shift) % mp, d) for d in range(mp)])

    def to_shift(array, shift):
        return lax.ppermute(array, "mp", [(d, (d + shift) % mp) for d in range(mp)])

    own_first = lambda a: jnp.roll(a[0], -at_mp * rows).astype(jnp.int32)
    seg, pad = own_first(seg_ids), own_first(pad_mask)
    fq, fk = mask_features(seg, pad)
    pad_row, pad_column = pad.reshape(1, seq_len), pad.reshape(seq_len, 1)
    turn = Turn()
    others = range(1, mp)

    piece = wo.shape[0] // dp
    wo_piece = lax.dynamic_slice_in_dim(wo, at_dp * piece, piece, 0)
    wo_pieces = [from_shift(wo_piece, shift) for shift in others]
    x, *wo_pieces = lax.optimization_barrier((x, *wo_pieces))
    x_parts = [x] + [from_shift(x, shift) for shift in others]
    wo_parts = [wo] + [lax.all_gather(got, "dp", axis=0, tiled=True) for got in wo_pieces]

    qkv, norm1_t = [], []
    for part in range(mp):
        if part == 1:
            grad, *x_parts[1:] = turn.join(grad, *x_parts[1:])
        got = project(turn, place, bits, x_parts[part], gain_attn, wq, wk, wv)
        qkv.append(got[0])
        norm1_t.append(got[1])
    g_parts = [grad] + [from_shift(grad, shift) for shift in others]

    total_pairs = cols // LANES
    group = max(1, total_pairs // 2)
    groups = [(first, group) for first in range(0, total_pairs, group)]

    ctx, qa, qb = attend(turn, qkv, fq, fk, pad_row)
    near = [from_shift(ctx[mp - shift], shift) for shift in others]
    far = [[from_shift(ctx[(part - shift) % mp], shift) for shift in others] for part in others]

    deep, norm2_t, grad_t, d_norm2, ffn_out = ([None] * mp for _ in range(5))
    for part in range(mp):
        contexts = [(array, 0) for array in [ctx[part], *(far[part - 1] if part else near)]]
        deep[part], ffn_out[part], d_norm2[part], norm2_t[part], grad_t[part], *kept = feed(
            turn, place, (bits, bits_other), x_parts[part], gain_ffn, g_parts[part],
            wo_parts, contexts, (wi0, wi1, wf), None if part else group * LANES,
        )
        if part == 0:
            h1, joined = kept
    dn_received = [to_shift(d_norm2[part], part) for part in others]
    *ffn_out[1:], last_received = lax.optimization_barrier((*ffn_out[1:], dn_received[-1]))
    dn_received[-1] = last_received
    ffn_received = [to_shift(ffn_out[part], part) for part in others]

    units = wi0.shape[1]
    cuts = [(0, 2)] if units % LANES == 0 else [(0, 1), (1, 1)]
    rights = [(array, 0) for array in deep]
    ffn_sides = [(norm2_t, rights, low, count) for low, count in cuts] + [(grad_t, rights, 2, 1)]
    ffn_orders = [bits] * len(cuts) + [bits_other]
    sent = weight_grads(turn, ffn_sides, 0, None)

    d_h1, dgain_ffn, branch_t, *d_ctx_all = middle(
        turn, place, bits, d_norm2[0], dn_received, h1, gain_ffn, grad, wo_parts
    )
    d_ctx = [d_ctx_all[0]] + [from_shift(d_ctx_all[mp - shift], shift) for shift in others]
    arrived = [swap(array, order[0]) for array, order in zip(turn.join(*sent), ffn_orders)]

    ffn_totals = weight_grads(turn, ffn_sides, 1, arrived)
    ffn_arrived = exchange(ffn_totals, ffn_orders, 1)

    stages = len(bits)

    def advance_ffn(at):
        nonlocal ffn_totals, ffn_arrived
        if at < stages:
            ffn_totals = halve(turn, ffn_totals, ffn_arrived)
            ffn_arrived = exchange(ffn_totals, ffn_orders, at)

    def advance(index, at):
        if at < stages:
            totals[index] = halve(turn, totals[index], waiting[index])
            waiting[index] = exchange(totals[index], [bits], at)

    grads, totals, waiting = [], [], []
    for index, (first, pairs) in enumerate(groups):
        got = attend_back(turn, qa, qb, qkv, fk, pad_column, ctx, d_ctx, first, pairs)
        grads.append(got)
        sides = [(norm1_t, [(got, part) for part in range(mp)], 0, 3)]
        if index == 0:
            sides.append(([branch_t], [(joined, 0)], 0, joined.shape[0]))
        sent = weight_grads(turn, sides, 0, None, True)
        arrived = [swap(array, bits[0]) for array in sent]
        advance_ffn(2 + index)
        if index == len(groups) - 1:
            dn_parts = [None] * mp
            for part in others:
                dn_parts[part] = dnorm1(turn, x_parts[part], grads, (wq, wk, wv), part)
            dn1_received = [to_shift(dn_parts[part][0], part) for part in others]
            dn_parts[0] = dnorm1(turn, x_parts[0], grads, (wq, wk, wv), 0)
            dgains = jnp.concatenate([sum(p[1] for p in dn_parts), dgain_ffn], axis=0)
            gains_arrived = swap(dgains, bits[0])
        totals.append(weight_grads(turn, sides, 1, arrived, True))
        if index == len(groups) - 1:
            dgains = dgains + turn.join(gains_arrived)[0]
            gains_arrived = swap(dgains, bits[1])
        waiting.append(exchange(totals[index], [bits], 1))

    layer_out = h1 + ffn_out[0].astype(F32)
    for received in ffn_received:
        layer_out = layer_out + received.astype(F32)
    layer_out = layer_out.astype(BF16)

    for at in range(2, stages):
        for index in range(len(groups)):
            if index == len(groups) - 1:
                dgains = dgains + turn.join(gains_arrived)[0]
                gains_arrived = swap(dgains, bits[at])
            advance(index, at)
    for at in range(2 + len(groups), stages):
        advance_ffn(at)
    d_x = last(turn, dn_parts[0][0], dn1_received, x, gain_attn, d_h1)
    dgains = dgains + turn.join(gains_arrived)[0]
    dgains = sum([dgains] + [from_shift(dgains, shift) for shift in others])
    ffn_totals = finish(ffn_totals, turn.join(*ffn_arrived))
    totals = [finish(total, turn.join(*came)) for total, came in zip(totals, waiting)]
    d_wi, d_wf = jnp.concatenate(ffn_totals[:-1], axis=1), ffn_totals[-1]
    wide = group * LANES
    pieces = [total[0][:, : 3 * wide].reshape(-1, 3, wide) for total in totals]
    d_wq, d_wk, d_wv = (
        jnp.concatenate([piece[:, which] for piece in pieces], axis=1) for which in range(3)
    )
    wo_grad = totals[0][0][:, 3 * wide :]
    d_wo = wo_grad[:, :cols]
    for shift in others:
        at = (mp - shift) * cols
        d_wo = d_wo + from_shift(wo_grad[:, at : at + cols].astype(BF16), shift).astype(F32)
    return (
        layer_out[None],
        d_x[None],
        d_wq,
        d_wk,
        d_wv,
        d_wo.T,
        d_wi[:, :units],
        d_wi[:, units:],
        d_wf.T,
        dgains[0],
        dgains[1],
    )


def solution(mesh):
    return jax.shard_map(
        per_device,
        mesh=mesh,
        in_specs=(
            P("dp", "mp", None),
            P("dp", None),
            P("dp", None),
            P(None, "mp"),
            P(None, "mp"),
            P(None, "mp"),
            P("mp", None),
            P(None, "mp"),
            P(None, "mp"),
            P("mp", None),
            P(),
            P(),
            P("dp", "mp", None),
        ),
        out_specs=(
            P("dp", "mp", None),
            P("dp", "mp", None),
            P("dp", "mp"),
            P("dp", "mp"),
            P("dp", "mp"),
            P("mp", "dp"),
            P("dp", "mp"),
            P("dp", "mp"),
            P("mp", "dp"),
            P(),
            P(),
        ),
        check_vma=False,
    )
```

```python
import functools

import jax
import jax.numpy as jnp
from jax import lax
from jax.experimental import pallas as pl
from jax.experimental.pallas import tpu as pltpu
from jax.sharding import PartitionSpec as P

HD = 64
LANES = 128
EPSILON = 1e-06
BIG = 2.0**30
F32 = jnp.float32
BF16 = jnp.bfloat16
NN = (((1,), (0,)), ((), ()))
NT = (((1,), (1,)), ((), ()))
MIB = 1 << 20
IN_HBM = ("attend", "weight_grads", "middle", "feed", "project", "attend_back", "dnorm1",)


def dot(lhs, rhs, dims=NN):
    return lax.dot_general(lhs, rhs, dims, preferred_element_type=F32)


class Turn:
    def __init__(self):
        self.token = jnp.zeros((1,), jnp.int32)

    def join(self, *arrays):
        self.token, *arrays = lax.optimization_barrier((self.token, *arrays))
        return arrays


def call(turn, kernel, name, grid, in_specs, out_specs, out_shape, args, flops, vmem, scratch=(), stay=False, pinned=(), weight=0.1):
    token_at = len(args) + len(out_shape)

    if stay:
        large = lambda a: a.size * a.dtype.itemsize > MIB // 4 and not any(a is b for b in pinned)
        args = [pltpu.with_memory_space_constraint(a, pltpu.HBM) if large(a) else a for a in args]

    placed = [
        pltpu.HBM(o.shape, o.dtype) if o.size * o.dtype.itemsize > MIB // 4 and name in IN_HBM else o for o in out_shape
    ]

    def with_token(token_ref, *refs):
        @pl.when(functools.reduce(lambda a, b: a & b, [pl.program_id(d) == 0 for d in range(len(grid))]))
        def _():
            refs[token_at][0] = 0

        kernel(*refs[:token_at], *refs[token_at + 1 :])

    *outs, turn.token = pl.pallas_call(
        with_token,
        grid=grid,
        in_specs=[pl.BlockSpec(memory_space=pl.ANY), *in_specs],
        out_specs=[*out_specs, pl.BlockSpec(memory_space=pltpu.SMEM)],
        out_shape=[*placed, shape((1,), jnp.int32)],
        scratch_shapes=list(scratch),
        compiler_params=pltpu.CompilerParams(vmem_limit_bytes=vmem * MIB),
        cost_estimate=pl.CostEstimate(
            flops=int(weight * flops),
            bytes_accessed=int(weight * sum(a.size * a.dtype.itemsize for a in (*args, *out_shape))),
            transcendentals=0,
        ),
        name=name,
    )(turn.token, *args)
    return outs


def pin(turn, *arrays):
    count = len(arrays)
    anywhere = pl.BlockSpec(memory_space=pl.ANY)

    def kernel(*refs):
        refs[-1][0] = 0

    *outs, turn.token = pl.pallas_call(
        kernel,
        in_specs=[anywhere] * (count + 1),
        out_specs=[anywhere] * count + [pl.BlockSpec(memory_space=pltpu.SMEM)],
        out_shape=[pltpu.VMEM(a.shape, a.dtype) for a in arrays] + [shape((1,), jnp.int32)],
        input_output_aliases={at + 1: at for at in range(count)},
        compiler_params=pltpu.CompilerParams(vmem_limit_bytes=4 * MIB),
        name="pin",
    )(turn.token, *[pltpu.with_memory_space_constraint(a, pltpu.VMEM) for a in arrays])
    return outs


def whole(array):
    zeros = (0,) * array.ndim
    return pl.BlockSpec(array.shape, lambda *_: zeros)


def shape(dims, dtype):
    return jax.ShapeDtypeStruct(dims, dtype)


SMEM_SPEC = pl.BlockSpec(memory_space=pltpu.SMEM)


def store_transposed(place_ref, values, out_ref, bits):
    turned = jnp.transpose(values)
    count = len(bits)
    rows = turned.shape[0] >> count
    for index in range(1 << count):
        target = 0
        for at, bit in enumerate(bits):
            own = 1 - (place_ref[bit] ^ ((index >> bit) & 1))
            target = target + own * (1 << (count - 1 - at))
        out_ref[pl.ds(pl.multiple_of(target * rows, rows), rows), :] = turned[
            index * rows : (index + 1) * rows
        ]


def project_kernel(bits, place, x_ref, gain_ref, wq_ref, wk_ref, wv_ref, qkv_ref, turned_ref):
    x = x_ref[...].astype(F32)
    inverse = lax.rsqrt(jnp.mean(x * x, axis=1, keepdims=True) + EPSILON)
    norm = (x * inverse * gain_ref[...]).astype(BF16)
    cols = wq_ref.shape[1]
    for index, weight in enumerate((wq_ref, wk_ref, wv_ref)):
        qkv_ref[:, index * cols : (index + 1) * cols] = dot(norm, weight[...]).astype(BF16)
    store_transposed(place, norm, turned_ref, bits)


def project(turn, place, bits, x, gain, wq, wk, wv):
    rows, width = x.shape
    block = min(256, rows)
    cols = wq.shape[1]
    return call(
        turn,
        functools.partial(project_kernel, bits),
        "project",
        (rows // block,),
        [
            SMEM_SPEC,
            pl.BlockSpec((block, width), lambda i: (i, 0)),
            whole(gain),
            whole(wq),
            whole(wk),
            whole(wv),
        ],
        [
            pl.BlockSpec((block, 3 * cols), lambda i: (i, 0)),
            pl.BlockSpec((width, block), lambda i: (0, i)),
        ],
        [shape((rows, 3 * cols), BF16), shape((width, rows), BF16)],
        (place, x, gain, wq, wk, wv),
        2.5 * rows * width * 3 * cols,
        20,
        stay=True,
    )


def mask_features(seg, pad):
    lane = jnp.arange(LANES) % HD
    same = seg[:, None] == lane[None, :]
    seg_lane = (lane < 6)[None, :]
    pad_lane = (lane == 6)[None, :]
    query = jnp.where(seg_lane & ~same, -BIG, 0.0) + jnp.where(pad_lane, -BIG, 0.0)
    key = jnp.where(seg_lane & same, 1.0, 0.0)
    key = key + jnp.where(pad_lane & (pad[:, None] == 0), 1.0, 0.0)
    key = key + jnp.where((lane >= 7) & (lane < 10), 1.0, 0.0)[None, :]
    return query.astype(BF16), key.astype(BF16)


def split3(values):
    high = values.astype(BF16)
    rest = values - high.astype(F32)
    middle = rest.astype(BF16)
    return high, middle, (rest - middle.astype(F32)).astype(BF16)


def rows_of(refs):
    return jnp.concatenate([ref[...] for ref in refs], axis=0)


def attend_kernel(parts, *refs):
    q_refs, k_refs, v_refs = refs[:parts], refs[parts : 2 * parts], refs[2 * parts : 3 * parts]
    fq_ref, fk_ref, pad_ref = refs[3 * parts : 3 * parts + 3]
    ctx_refs, (qa_ref, qb_ref) = refs[3 * parts + 3 : -2], refs[-2:]
    q = rows_of(q_refs) * BF16(HD**-0.5)
    k = rows_of(k_refs)
    v = rows_of(v_refs)
    block = q.shape[0]
    low = lax.broadcasted_iota(jnp.int32, q.shape, 1) < HD
    row = lax.broadcasted_iota(jnp.int32, (LANES, block), 0)
    upper = row < HD
    inner = row & (HD - 1)
    fq = fq_ref[...]
    fk = fk_ref[...]
    v_t = jnp.transpose(v)
    one = jnp.ones((), BF16)
    v_own = v_t.astype(F32)
    product = jnp.transpose(q.astype(F32) * k.astype(F32))
    padded = pad_ref[...] == 0
    outs, log_totals = [], []
    for head in range(2):
        first = head == 0
        q_head = jnp.where(low, q, fq) if first else jnp.where(low, fq, q)
        k_head = jnp.where(low, k, fk) if first else jnp.where(low, fk, k)
        v_head = jnp.where(upper, v_t, one) if first else jnp.where(upper, one, v_t)
        mine = upper if first else ~upper
        own = jnp.sum(product[head * HD : head * HD + HD], axis=0, keepdims=True)
        own = jnp.where(padded, own, -1e30)
        scores = dot(k_head, q_head, NT)
        top = jnp.maximum(jnp.max(scores, axis=0, keepdims=True), own)
        expo = jnp.exp(scores - top).astype(BF16)
        both = dot(v_head, expo) + jnp.exp(own - top) * jnp.where(mine, v_own, 1.0)
        total = both[HD : HD + 1] if first else both[0:1]
        outs.append(both / total)
        log_totals.append(split3(-(top + jnp.log(total))))
    context = jnp.transpose(jnp.where(upper, outs[0], outs[1])).astype(BF16)
    rows = block // parts
    for part, ctx_ref in enumerate(ctx_refs):
        ctx_ref[...] = context[part * rows : (part + 1) * rows]
    extra = jnp.zeros((LANES, block), F32)
    for at in range(3):
        piece = jnp.where(upper, log_totals[1][at].astype(F32), log_totals[0][at].astype(F32))
        extra = jnp.where(inner == 7 + at, piece, extra)
    fq = fq + jnp.transpose(extra).astype(BF16)
    qa_ref[...] = jnp.where(low, q, fq)
    qb_ref[...] = jnp.where(low, fq, q)


def attend(turn, qkv, fq, fk, pad):
    parts = len(qkv)
    rows, cols = qkv[0].shape[0], qkv[0].shape[1] // 3
    seq_len = parts * rows
    pairs = cols // LANES
    at = lambda which: [pl.BlockSpec((rows, LANES), lambda p: (0, which * pairs + p))] * parts
    tall = pl.BlockSpec((seq_len, LANES), lambda p: (0, p))
    part = pl.BlockSpec((rows, LANES), lambda p: (0, p))
    *ctx, qa, qb = call(
        turn,
        functools.partial(attend_kernel, parts),
        "attend",
        (pairs,),
        at(0) + at(1) + at(2) + [whole(fq), whole(fk), whole(pad)],
        [part] * parts + [tall] * 2,
        [shape((rows, pairs * LANES), BF16)] * parts + [shape((seq_len, pairs * LANES), BF16)] * 2,
        (*qkv, *qkv, *qkv, fq, fk, pad),
        4000 * seq_len * seq_len * pairs,
        40,
        stay=True,
    )
    return ctx, qa, qb


def attend_back_kernel(parts, qa_ref, qb_ref, fk_ref, pad_ref, *refs):
    *refs, out_ref = refs
    k, v, ctx, dctx = (rows_of(refs[at * parts : (at + 1) * parts]) for at in range(4))
    lane = lax.broadcasted_iota(jnp.int32, k.shape, 1)
    low = lane < HD
    inner = lane & (HD - 1)
    fk = fk_ref[...]
    k_own = k.astype(F32)
    dctx_f = dctx.astype(F32)
    product = dctx_f * ctx.astype(F32)
    product_v = dctx_f * v.astype(F32)
    padded = pad_ref[...] == 0
    one = jnp.ones((), BF16)
    zero = jnp.zeros((), BF16)
    dctx_t = jnp.transpose(dctx)
    dq, dk, dv = [], [], []
    for head in range(2):
        mine = low if head == 0 else ~low
        span = slice(head * HD, head * HD + HD)
        q_head = (qa_ref if head == 0 else qb_ref)[...]
        k_head = jnp.where(mine, k, fk)
        v_head = jnp.where(mine, v, one)
        delta = jnp.sum(jnp.where(mine, product, 0.0), axis=1, keepdims=True)
        high, middle, rest = split3(-delta)
        extra = jnp.where(inner == 0, high, jnp.where(inner == 1, middle, jnp.where(inner == 2, rest, zero)))
        weights = jnp.exp(dot(q_head, k_head, NT))
        d_raw = (weights * dot(jnp.where(mine, dctx, extra), v_head, NT)).astype(BF16)
        q_f = q_head.astype(F32)
        lifted = jnp.sum(jnp.where(~mine & (inner >= 7) & (inner < 10), q_f, 0.0), axis=1, keepdims=True)
        own = jnp.sum(jnp.where(mine, q_f * k_own, 0.0), axis=1, keepdims=True) + lifted
        w_own = jnp.where(padded, jnp.exp(jnp.where(padded, own, 0.0)), 0.0)
        d_own = w_own * (jnp.sum(jnp.where(mine, product_v, 0.0), axis=1, keepdims=True) - delta)
        dq.append(dot(d_raw, k) + d_own * k_own)
        dk.append((dot(jnp.transpose(q_head)[span], d_raw), d_own * q_f))
        dv.append((dot(dctx_t[span], weights.astype(BF16)), w_own * dctx_f))
    out_ref[0] = (jnp.where(low, dq[0], dq[1]) * HD**-0.5).astype(BF16)
    for at, parts in ((1, dk), (2, dv)):
        main = jnp.transpose(jnp.concatenate([parts[0][0], parts[1][0]], axis=0))
        out_ref[at] = (main + jnp.where(low, parts[0][1], parts[1][1])).astype(BF16)


def attend_back(turn, qa, qb, qkv, fk, pad, ctx, dctx, first, pairs):
    parts = len(qkv)
    rows, cols = qkv[0].shape[0], qkv[0].shape[1] // 3
    seq_len = parts * rows
    total = cols // LANES
    tall = pl.BlockSpec((seq_len, LANES), lambda p: (0, first + p))
    part = [pl.BlockSpec((rows, LANES), lambda p: (0, first + p))] * parts
    at = lambda which: [pl.BlockSpec((rows, LANES), lambda p: (0, which * total + first + p))] * parts
    return call(
        turn,
        functools.partial(attend_back_kernel, parts),
        "attend_back",
        (pairs,),
        [tall, tall, whole(fk), whole(pad)] + at(1) + at(2) + part + at(0),
        [pl.BlockSpec((3, seq_len, LANES), lambda p: (0, 0, p))],
        [shape((3, seq_len, pairs * LANES), BF16)],
        (qa, qb, fk, pad, *qkv, *qkv, *ctx, *dctx),
        6700 * seq_len * seq_len * pairs,
        44,
        stay=True,
        weight=0.5 if first == 0 else 0.1,
    )[0]


def feed_kernel(bits, counts, place, x_ref, gain_ref, g_ref, *refs):
    heads, groups, own = counts
    wo_refs, refs = refs[:heads], refs[heads:]
    ctx_refs, refs = refs[:groups], refs[groups:]
    (wi0_ref, wi1_ref, wf_ref), refs = refs[:3], refs[3:]
    deep_ref, out_ref, dnorm_ref, norm_t_ref, grad_t_ref = refs[:5]
    context = jnp.concatenate([ctx[...] for ctx in ctx_refs], axis=1)
    h1 = x_ref[...].astype(F32)
    at = 0
    for wo_ref in wo_refs:
        h1 = h1 + dot(context[:, at : at + wo_ref.shape[0]], wo_ref[...])
        at += wo_ref.shape[0]
    if own:
        h1_ref, joined_ref = refs[5:7]
        h1_ref[...] = h1
        for at in range(joined_ref.shape[0]):
            joined_ref[at] = context[:, at * joined_ref.shape[2] : (at + 1) * joined_ref.shape[2]]
    inverse = lax.rsqrt(jnp.mean(h1 * h1, axis=1, keepdims=True) + EPSILON)
    norm = (h1 * inverse * gain_ref[...]).astype(BF16)
    grad = g_ref[...]
    store_transposed(place, norm, norm_t_ref, bits[0])
    store_transposed(place, grad, grad_t_ref, bits[1])

    gate = dot(norm, wi0_ref[...])
    up = dot(norm, wi1_ref[...])
    d_hidden = dot(grad, wf_ref[...], NT)
    slope = 0.7978845608028654
    square = gate * gate
    curve = jnp.tanh(slope * gate * (1.0 + 0.044715 * square))
    half = 0.5 * (1.0 + curve)
    active = gate * half
    d_active = half + 0.5 * gate * (1.0 - curve * curve) * (slope + (3.0 * 0.044715 * slope) * square)
    hidden = (active * up).astype(BF16)
    d_gate = (d_hidden * up * d_active).astype(BF16)
    d_up = (d_hidden * active).astype(BF16)
    deep_ref[0] = d_gate
    deep_ref[1] = d_up
    deep_ref[2] = hidden
    dnorm_ref[...] = (dot(d_gate, wi0_ref[...], NT) + dot(d_up, wi1_ref[...], NT)).astype(BF16)
    out_ref[...] = dot(hidden, wf_ref[...]).astype(BF16)


def feed(turn, place, bits, x, gain, grad, wo_parts, contexts, weights, own):
    rows, width = x.shape
    units = weights[0].shape[1]
    block = min(256, rows)
    steps = rows // block
    columns = sum(array.shape[1] for array, _ in contexts)
    wide = pl.BlockSpec((block, width), lambda i: (i, 0))
    tall = pl.BlockSpec((width, block), lambda i: (0, i))
    ctx_specs = [
        pl.BlockSpec((block, array.shape[1]), functools.partial(lambda at, i: (at * steps + i, 0), at))
        for array, at in contexts
    ]
    out_specs = [pl.BlockSpec((3, block, units), lambda i: (0, i, 0)), wide, wide, tall, tall]
    out_shapes = (
        [shape((3, rows, units), BF16)]
        + [shape((rows, width), BF16)] * 2
        + [shape((width, rows), BF16)] * 2
    )
    if own:
        out_specs += [wide, pl.BlockSpec((columns // own, block, own), lambda i: (0, i, 0))]
        out_shapes += [shape((rows, width), F32), shape((columns // own, rows, own), BF16)]
    kernel = functools.partial(feed_kernel, bits, (len(wo_parts), len(contexts), own))
    return call(
        turn,
        kernel,
        "feed",
        (steps,),
        [SMEM_SPEC, wide, whole(gain), wide]
        + [whole(w) for w in wo_parts]
        + ctx_specs
        + [pl.BlockSpec(memory_space=pltpu.VMEM)] * 3,
        out_specs,
        out_shapes,
        (place, x, gain, grad, *wo_parts, *[array for array, _ in contexts], *weights),
        rows * width * (15 * units + 2.5 * columns),
        40,
        pinned=weights,
        stay=True,
    )


def middle_kernel(bits, heads, place, dn_ref, h1_ref, gain_ref, g_ref, *refs):
    wo_refs, refs = refs[:heads], refs[heads:]
    recv_refs, (dh_ref, dgain_ref, turned_ref, *dctx_refs) = refs[: -3 - heads], refs[-3 - heads :]
    d_norm = dn_ref[...].astype(F32)
    for recv in recv_refs:
        d_norm = d_norm + recv[...].astype(F32)
    h1 = h1_ref[...]
    inverse = lax.rsqrt(jnp.mean(h1 * h1, axis=1, keepdims=True) + EPSILON)
    normed = h1 * inverse
    scaled = gain_ref[...] * d_norm
    d_h1 = g_ref[...].astype(F32) + inverse * (
        scaled - normed * jnp.mean(scaled * normed, axis=1, keepdims=True)
    )
    dh_ref[...] = d_h1
    branch = d_h1.astype(BF16)
    for wo_ref, dctx_ref in zip(wo_refs, dctx_refs):
        dctx_ref[...] = dot(branch, wo_ref[...], NT).astype(BF16)
    store_transposed(place, branch, turned_ref, bits)

    @pl.when(pl.program_id(0) == 0)
    def _():
        dgain_ref[...] = jnp.zeros_like(dgain_ref)

    dgain_ref[...] += jnp.sum(d_norm * normed, axis=0, keepdims=True)


def middle(turn, place, bits, d_norm, received, h1, gain, grad, wo_parts):
    rows, width = h1.shape
    block = min(256, rows)
    heads = len(wo_parts)
    wide = pl.BlockSpec((block, width), lambda i: (i, 0))
    return call(
        turn,
        functools.partial(middle_kernel, bits, heads),
        "middle",
        (rows // block,),
        [SMEM_SPEC, wide, wide, whole(gain), wide] + [whole(w) for w in wo_parts] + [wide] * len(received),
        [wide, pl.BlockSpec((1, width), lambda i: (0, 0)), pl.BlockSpec((width, block), lambda i: (0, i))]
        + [pl.BlockSpec((block, w.shape[0]), lambda i: (i, 0)) for w in wo_parts],
        [shape((rows, width), F32), shape((1, width), F32), shape((width, rows), BF16)]
        + [shape((rows, w.shape[0]), BF16) for w in wo_parts],
        (place, d_norm, h1, gain, grad, *wo_parts, *received),
        2.5 * rows * width * sum(w.shape[0] for w in wo_parts),
        20,
        weight=0.1,
    )


def dnorm1(turn, x, grads, weights, part):
    rows, width = x.shape
    block = min(256, rows)
    steps = rows // block
    count = len(grads)

    def kernel(x_ref, *refs):
        grad_refs, w_refs, (dn_ref, dgain_ref) = refs[:count], refs[count:-2], refs[-2:]
        d_norm = None
        for group, g_ref in enumerate(grad_refs):
            size = g_ref.shape[2]
            for which, w_ref in enumerate(w_refs):
                term = dot(g_ref[which], w_ref[:, group * size : (group + 1) * size], NT)
                d_norm = term if d_norm is None else d_norm + term
        dn_ref[...] = d_norm.astype(BF16)
        x = x_ref[...].astype(F32)
        inverse = lax.rsqrt(jnp.mean(x * x, axis=1, keepdims=True) + EPSILON)

        @pl.when(pl.program_id(0) == 0)
        def _():
            dgain_ref[...] = jnp.zeros_like(dgain_ref)

        dgain_ref[...] += jnp.sum(d_norm * (x * inverse), axis=0, keepdims=True)

    wide = pl.BlockSpec((block, width), lambda i: (i, 0))
    return call(
        turn,
        kernel,
        "dnorm1",
        (steps,),
        [wide]
        + [pl.BlockSpec((3, block, g.shape[2]), lambda i: (0, part * steps + i, 0)) for g in grads]
        + [whole(w) for w in weights],
        [wide, pl.BlockSpec((1, width), lambda i: (0, 0))],
        [shape((rows, width), BF16), shape((1, width), F32)],
        (x, *grads, *weights),
        2.5 * rows * width * 3 * weights[0].shape[1],
        20,
    )


def last_kernel(dn_ref, x_ref, gain_ref, dh_ref, *rest):
    recv_refs, dx_ref = rest[:-1], rest[-1]
    d_norm = dn_ref[...].astype(F32)
    for recv in recv_refs:
        d_norm = d_norm + recv[...].astype(F32)
    x = x_ref[...].astype(F32)
    inverse = lax.rsqrt(jnp.mean(x * x, axis=1, keepdims=True) + EPSILON)
    normed = x * inverse
    scaled = gain_ref[...] * d_norm
    dx_ref[...] = dh_ref[...] + inverse * (
        scaled - normed * jnp.mean(scaled * normed, axis=1, keepdims=True)
    )


def last(turn, d_norm, received, x, gain, d_h1):
    rows, width = x.shape
    block = min(256, rows)
    wide = pl.BlockSpec((block, width), lambda i: (i, 0))
    return call(
        turn,
        last_kernel,
        "last",
        (rows // block,),
        [wide, wide, whole(gain), wide] + [wide] * len(received),
        [wide],
        [shape((rows, width), F32)],
        (d_norm, x, gain, d_h1, *received),
        100 * rows * width,
        20,
    )[0]


def weight_grads(turn, sides, start, received, joint=False, stay=False):
    count = sides[0][0][0].shape[0] // 2
    received = received or []
    cuts = 2 if received else 1
    lefts = [left for side in sides for left in side[0]]
    rights, right_specs, spans = [], [], []
    for lefts_of, rights_of, lowest, weights in sides:
        first = spans[-1][1] if spans else 0
        columns = rights_of[0][0].shape[2]
        spans.append((first, first + weights))
        for left, (right, at) in zip(lefts_of, rights_of):
            rights.append(right)
            right_specs.append(
                pl.BlockSpec(
                    (1, left.shape[1], columns),
                    functools.partial(
                        lambda f, n, low, at, w: (low + jnp.clip(w - f, 0, n - 1), at, 0),
                        first, weights, lowest, at,
                    ),
                )
            )

    wholes = [(0, spans[-1][1])] if joint else spans
    outputs = len(wholes)

    def kernel(*refs):
        left_refs = refs[: len(lefts)]
        right_refs = refs[len(lefts) : len(lefts) + len(rights)]
        recv_refs = refs[len(lefts) + len(rights) : len(refs) - cuts * outputs]
        out_refs = refs[len(refs) - cuts * outputs :]
        weight = pl.program_id(0)
        at = 0
        for side, (first, last) in enumerate(spans):

            @pl.when((weight >= first) & (weight < last))
            def _(side=side, at=at):
                out = 0 if joint else side
                total = recv_refs[out][...].astype(F32) if recv_refs else None
                for part in range(at, at + len(sides[side][0])):
                    term = dot(left_refs[part][...], right_refs[part][0])
                    total = term if total is None else total + term
                rows = count // cuts
                for cut in range(cuts):
                    out_refs[out * cuts + cut][...] = total[cut * rows : (cut + 1) * rows].astype(BF16)

            at += len(sides[side][0])

    widths = [side[1][0][0].shape[2] for side in sides][:outputs]

    def specs(rows):
        return [
            pl.BlockSpec(
                (rows, columns),
                functools.partial(lambda f, n, w: (0, jnp.clip(w - f, 0, n - 1)), first, last - first),
            )
            for columns, (first, last) in zip(widths, wholes)
        ]

    out_specs, out_shapes = [], []
    for spec, columns, (first, last) in zip(specs(count // cuts), widths, wholes):
        out_specs += [spec] * cuts
        out_shapes += [shape((count // cuts, (last - first) * columns), BF16)] * cuts
    outs = call(
        turn,
        kernel,
        "weight_grads",
        (spans[-1][1],),
        [pl.BlockSpec((count, left.shape[1]), lambda w: (start, 0)) for left in lefts]
        + right_specs
        + (specs(count) if received else []),
        out_specs,
        out_shapes,
        (*lefts, *rights, *received),
        2.5 * count * sum(side[3] * side[1][0][0].shape[2] * l.shape[1] for side in sides for l in side[0]),
        28,
        stay=stay,
    )
    return [tuple(outs[at : at + 2]) for at in range(0, len(outs), 2)] if received else outs


def add(left, right):
    return (left.astype(F32) + right.astype(F32)).astype(BF16)


def swap(array, bit):
    size = lax.axis_size("dp")
    return lax.ppermute(array, "dp", [(i, i ^ (1 << bit)) for i in range(size)])


def halve(turn, totals, arrived):
    outs = []
    arrived = turn.join(*arrived)
    for (_, kept), came in zip(totals, arrived):
        cut = kept.shape[0] // 2
        outs.append((add(kept[:cut], came[:cut]), add(kept[cut:], came[cut:])))
    flat = turn.join(*[part for pair in outs for part in pair])
    return list(zip(flat[::2], flat[1::2]))


def finish(totals, arrived):
    return [kept.astype(F32) + came.astype(F32) for (_, kept), came in zip(totals, arrived)]


def exchange(totals, orders, at):
    return [swap(send, order[at]) for (send, _), order in zip(totals, orders)]


def per_device(
    layer_in, seg_ids, pad_mask, wq, wk, wv, wo, wi0, wi1, wf, gain_attn, gain_ffn, out_grad
):
    dp, mp = lax.axis_size("dp"), lax.axis_size("mp")
    at_dp, at_mp = lax.axis_index("dp"), lax.axis_index("mp")
    bits = tuple(range(dp.bit_length() - 1))
    bits_other = bits[:1] + bits[2:3] + bits[1:2] + bits[3:]
    place = jnp.stack([(at_dp >> bit) & 1 for bit in bits]).astype(jnp.int32)
    seq_len = seg_ids.shape[1]
    x = layer_in[0]
    grad = out_grad[0]
    rows, width = x.shape
    cols = wq.shape[1]
    gain_attn = gain_attn.reshape(1, width)
    gain_ffn = gain_ffn.reshape(1, width)

    def from_shift(array, shift):
        return lax.ppermute(array, "mp", [((d + shift) % mp, d) for d in range(mp)])

    def to_shift(array, shift):
        return lax.ppermute(array, "mp", [(d, (d + shift) % mp) for d in range(mp)])

    own_first = lambda a: jnp.roll(a[0], -at_mp * rows).astype(jnp.int32)
    seg, pad = own_first(seg_ids), own_first(pad_mask)
    fq, fk = mask_features(seg, pad)
    pad_row, pad_column = pad.reshape(1, seq_len), pad.reshape(seq_len, 1)
    turn = Turn()
    others = range(1, mp)

    piece = wo.shape[0] // dp
    wo_piece = lax.dynamic_slice_in_dim(wo, at_dp * piece, piece, 0)
    x, wo_piece = lax.optimization_barrier((x, wo_piece))
    wo_pieces = [from_shift(wo_piece, shift) for shift in others]
    x_parts = [x] + [from_shift(x, shift) for shift in others]

    qkv, norm1_t = [], []
    for part in range(mp):
        if part == 1:
            wo_parts = [wo]
            for got in turn.join(*wo_pieces):
                wo_parts.append(lax.all_gather(got, "dp", axis=0, tiled=True))
            grad, *x_parts[1:] = turn.join(grad, *x_parts[1:])
        got = project(turn, place, bits, x_parts[part], gain_attn, wq, wk, wv)
        qkv.append(got[0])
        norm1_t.append(got[1])
    g_parts = [grad] + [from_shift(grad, shift) for shift in others]

    total_pairs = cols // LANES
    group = max(1, total_pairs // 2)
    groups = [(first, group) for first in range(0, total_pairs, group)]

    ctx, qa, qb = attend(turn, qkv, fq, fk, pad_row)
    near = [from_shift(ctx[mp - shift], shift) for shift in others]
    weights = pin(turn, wi0, wi1, wf)
    far = [[from_shift(ctx[(part - shift) % mp], shift) for shift in others] for part in others]

    deep, norm2_t, grad_t, d_norm2, ffn_out = ([None] * mp for _ in range(5))
    for part in range(mp):
        contexts = [(array, 0) for array in [ctx[part], *(far[part - 1] if part else near)]]
        deep[part], ffn_out[part], d_norm2[part], norm2_t[part], grad_t[part], *kept = feed(
            turn, place, (bits, bits_other), x_parts[part], gain_ffn, g_parts[part],
            wo_parts, contexts, weights, None if part else group * LANES,
        )
        if part == 0:
            h1, joined = kept
    dn_received = [to_shift(d_norm2[part], part) for part in others]
    *ffn_out[1:], last_received = lax.optimization_barrier((*ffn_out[1:], dn_received[-1]))
    dn_received[-1] = last_received
    ffn_received = [to_shift(ffn_out[part], part) for part in others]

    deep = pin(turn, *deep)
    units = wi0.shape[1]
    cuts = [(0, 2)] if units % LANES == 0 else [(0, 1), (1, 1)]
    rights = [(array, 0) for array in deep]
    ffn_sides = [(norm2_t, rights, low, count) for low, count in cuts] + [(grad_t, rights, 2, 1)]
    ffn_orders = [bits] * len(cuts) + [bits_other]
    sent = weight_grads(turn, ffn_sides, 0, None)
    held = lax.optimization_barrier((*sent, *dn_received))
    sent, dn_received = held[: len(sent)], list(held[len(sent) :])
    arrived = [swap(array, order[0]) for array, order in zip(sent, ffn_orders)]

    d_h1, dgain_ffn, branch_t, *d_ctx_all = middle(
        turn, place, bits, d_norm2[0], dn_received, h1, gain_ffn, grad, wo_parts
    )
    d_ctx = [d_ctx_all[0]] + [from_shift(d_ctx_all[mp - shift], shift) for shift in others]

    ffn_totals = weight_grads(turn, ffn_sides, 1, arrived)
    ffn_arrived = exchange(ffn_totals, ffn_orders, 1)

    stages = len(bits)

    def advance_ffn(at):
        nonlocal ffn_totals, ffn_arrived
        if at < stages:
            ffn_totals = halve(turn, ffn_totals, ffn_arrived)
            ffn_arrived = exchange(ffn_totals, ffn_orders, at)

    def advance(index, at):
        if at < stages:
            totals[index] = halve(turn, totals[index], waiting[index])
            waiting[index] = exchange(totals[index], [bits], at)

    grads, totals, waiting = [], [], []
    tail = len(groups) - 1
    dn_parts = [None] * mp
    for index, (first, pairs) in enumerate(groups):
        got = attend_back(turn, qa, qb, qkv, fk, pad_column, ctx, d_ctx, first, pairs)
        grads.append(got)
        sides = [(norm1_t, [(got, part) for part in range(mp)], 0, 3)]
        if index == 0:
            sides.append(([branch_t], [(joined, 0)], 0, joined.shape[0]))
        sent = weight_grads(turn, sides, 0, None, True)
        arrived = [swap(array, bits[0]) for array in sent]
        if index == 0:
            advance_ffn(2)
            if not tail:
                advance_ffn(3)
        if index == tail:
            if tail:
                advance(0, 2)
                advance_ffn(3)
            for part in others:
                dn_parts[part] = dnorm1(turn, x_parts[part], grads, (wq, wk, wv), part)
            dn1_received = [to_shift(dn_parts[part][0], part) for part in others]
        totals.append(weight_grads(turn, sides, 1, arrived, True))
        waiting.append(exchange(totals[index], [bits], 1))
    dn_parts[0] = dnorm1(turn, x_parts[0], grads, (wq, wk, wv), 0)
    dgains = jnp.concatenate([sum(p[1] for p in dn_parts), dgain_ffn], axis=0)
    gains_arrived = swap(dgains, bits[0])
    if tail:
        advance(0, 3)

    layer_out = h1 + ffn_out[0].astype(F32)
    for received in turn.join(*ffn_received):
        layer_out = layer_out + received.astype(F32)
    layer_out = layer_out.astype(BF16)

    for at in range(2, stages):
        gains_came, *waiting[tail] = turn.join(gains_arrived, *waiting[tail])
        dgains = dgains + gains_came
        gains_arrived = swap(dgains, bits[at - 1])
        advance(tail, at)
    for at in range(4, stages):
        if tail:
            advance(0, at)
        advance_ffn(at)
    dgains = dgains + turn.join(gains_arrived)[0]
    gains_arrived = swap(dgains, bits[-1])
    wide = group * LANES
    ffn_totals = finish(ffn_totals, turn.join(*ffn_arrived))
    wo_grad = finish(totals[0], turn.join(*waiting[0]))[0][:, 3 * wide :]
    wo_arrived = [
        from_shift(wo_grad[:, (mp - shift) * cols : (mp - shift + 1) * cols].astype(BF16), shift)
        for shift in others
    ]
    dgains = dgains + turn.join(gains_arrived)[0]
    gains_parts = [dgains] + [from_shift(dgains, shift) for shift in others]
    d_x = last(turn, dn_parts[0][0], dn1_received, x, gain_attn, d_h1)
    totals = [finish(total, turn.join(*came)) for total, came in zip(totals, waiting)]
    d_wo = wo_grad[:, :cols]
    for array in turn.join(*wo_arrived):
        d_wo = d_wo + array.astype(F32)
    dgains = sum(turn.join(*gains_parts)) + turn.token.astype(F32)
    d_wi, d_wf = jnp.concatenate(ffn_totals[:-1], axis=1), ffn_totals[-1]
    pieces = [total[0][:, : 3 * wide].reshape(-1, 3, wide) for total in totals]
    d_wq, d_wk, d_wv = (
        jnp.concatenate([piece[:, which] for piece in pieces], axis=1) for which in range(3)
    )
    return (
        layer_out[None],
        d_x[None],
        d_wq,
        d_wk,
        d_wv,
        d_wo.T,
        d_wi[:, :units],
        d_wi[:, units:],
        d_wf.T,
        dgains[0],
        dgains[1],
    )


def solution(mesh):
    return jax.shard_map(
        per_device,
        mesh=mesh,
        in_specs=(
            P("dp", "mp", None),
            P("dp", None),
            P("dp", None),
            P(None, "mp"),
            P(None, "mp"),
            P(None, "mp"),
            P("mp", None),
            P(None, "mp"),
            P(None, "mp"),
            P("mp", None),
            P(),
            P(),
            P("dp", "mp", None),
        ),
        out_specs=(
            P("dp", "mp", None),
            P("dp", "mp", None),
            P("dp", "mp"),
            P("dp", "mp"),
            P("dp", "mp"),
            P("mp", "dp"),
            P("dp", "mp"),
            P("dp", "mp"),
            P("mp", "dp"),
            P(),
            P(),
        ),
        check_vma=False,
    )
```

```python
import functools

import jax
import jax.numpy as jnp
from jax import lax
from jax.experimental import pallas as pl
from jax.experimental.pallas import tpu as pltpu
from jax.sharding import PartitionSpec as P

HD = 64
LANES = 128
EPSILON = 1e-06
BIG = 2.0**30
F32 = jnp.float32
BF16 = jnp.bfloat16
NN = (((1,), (0,)), ((), ()))
NT = (((1,), (1,)), ((), ()))
MIB = 1 << 20
IN_HBM = ("attend", "weight_grads", "middle", "feed", "project", "attend_back", "dnorm1",)


def dot(lhs, rhs, dims=NN):
    return lax.dot_general(lhs, rhs, dims, preferred_element_type=F32)


class Turn:
    def __init__(self):
        self.token = jnp.zeros((1,), jnp.int32)

    def join(self, *arrays):
        self.token, *arrays = lax.optimization_barrier((self.token, *arrays))
        return arrays


def call(turn, kernel, name, grid, in_specs, out_specs, out_shape, args, flops, vmem, scratch=(), stay=False, pinned=(), weight=0.1):
    token_at = len(args) + len(out_shape)

    if stay:
        large = lambda a: a.size * a.dtype.itemsize > MIB // 4 and not any(a is b for b in pinned)
        args = [pltpu.with_memory_space_constraint(a, pltpu.HBM) if large(a) else a for a in args]

    placed = [
        pltpu.HBM(o.shape, o.dtype) if o.size * o.dtype.itemsize > MIB // 4 and name in IN_HBM else o for o in out_shape
    ]

    def with_token(token_ref, *refs):
        @pl.when(functools.reduce(lambda a, b: a & b, [pl.program_id(d) == 0 for d in range(len(grid))]))
        def _():
            refs[token_at][0] = 0

        kernel(*refs[:token_at], *refs[token_at + 1 :])

    *outs, turn.token = pl.pallas_call(
        with_token,
        grid=grid,
        in_specs=[pl.BlockSpec(memory_space=pl.ANY), *in_specs],
        out_specs=[*out_specs, pl.BlockSpec(memory_space=pltpu.SMEM)],
        out_shape=[*placed, shape((1,), jnp.int32)],
        scratch_shapes=list(scratch),
        compiler_params=pltpu.CompilerParams(vmem_limit_bytes=vmem * MIB),
        cost_estimate=pl.CostEstimate(
            flops=int(weight * flops),
            bytes_accessed=int(weight * sum(a.size * a.dtype.itemsize for a in (*args, *out_shape))),
            transcendentals=0,
        ),
        name=name,
    )(turn.token, *args)
    return outs


def pin(turn, *arrays):
    count = len(arrays)
    anywhere = pl.BlockSpec(memory_space=pl.ANY)

    def kernel(*refs):
        refs[-1][0] = 0

    *outs, turn.token = pl.pallas_call(
        kernel,
        in_specs=[anywhere] * (count + 1),
        out_specs=[anywhere] * count + [pl.BlockSpec(memory_space=pltpu.SMEM)],
        out_shape=[pltpu.VMEM(a.shape, a.dtype) for a in arrays] + [shape((1,), jnp.int32)],
        input_output_aliases={at + 1: at for at in range(count)},
        compiler_params=pltpu.CompilerParams(vmem_limit_bytes=4 * MIB),
        name="pin",
    )(turn.token, *[pltpu.with_memory_space_constraint(a, pltpu.VMEM) for a in arrays])
    return outs


def whole(array):
    zeros = (0,) * array.ndim
    return pl.BlockSpec(array.shape, lambda *_: zeros)


def shape(dims, dtype):
    return jax.ShapeDtypeStruct(dims, dtype)


SMEM_SPEC = pl.BlockSpec(memory_space=pltpu.SMEM)


def store_transposed(place_ref, values, out_ref, bits):
    turned = jnp.transpose(values)
    count = len(bits)
    rows = turned.shape[0] >> count
    for index in range(1 << count):
        target = 0
        for at, bit in enumerate(bits):
            own = 1 - (place_ref[bit] ^ ((index >> bit) & 1))
            target = target + own * (1 << (count - 1 - at))
        out_ref[pl.ds(pl.multiple_of(target * rows, rows), rows), :] = turned[
            index * rows : (index + 1) * rows
        ]


def project_kernel(bits, place, x_ref, gain_ref, wq_ref, wk_ref, wv_ref, qkv_ref, turned_ref):
    x = x_ref[...].astype(F32)
    inverse = lax.rsqrt(jnp.mean(x * x, axis=1, keepdims=True) + EPSILON)
    norm = (x * inverse * gain_ref[...]).astype(BF16)
    cols = wq_ref.shape[1]
    for index, weight in enumerate((wq_ref, wk_ref, wv_ref)):
        qkv_ref[:, index * cols : (index + 1) * cols] = dot(norm, weight[...]).astype(BF16)
    store_transposed(place, norm, turned_ref, bits)


def project(turn, place, bits, x, gain, wq, wk, wv):
    rows, width = x.shape
    block = min(256, rows)
    cols = wq.shape[1]
    return call(
        turn,
        functools.partial(project_kernel, bits),
        "project",
        (rows // block,),
        [
            SMEM_SPEC,
            pl.BlockSpec((block, width), lambda i: (i, 0)),
            whole(gain),
            whole(wq),
            whole(wk),
            whole(wv),
        ],
        [
            pl.BlockSpec((block, 3 * cols), lambda i: (i, 0)),
            pl.BlockSpec((width, block), lambda i: (0, i)),
        ],
        [shape((rows, 3 * cols), BF16), shape((width, rows), BF16)],
        (place, x, gain, wq, wk, wv),
        2.5 * rows * width * 3 * cols,
        20,
        stay=True,
    )


def mask_features(seg, pad):
    lane = jnp.arange(LANES) % HD
    same = seg[:, None] == lane[None, :]
    seg_lane = (lane < 6)[None, :]
    pad_lane = (lane == 6)[None, :]
    query = jnp.where(seg_lane & ~same, -BIG, 0.0) + jnp.where(pad_lane, -BIG, 0.0)
    key = jnp.where(seg_lane & same, 1.0, 0.0)
    key = key + jnp.where(pad_lane & (pad[:, None] == 0), 1.0, 0.0)
    key = key + jnp.where((lane >= 7) & (lane < 10), 1.0, 0.0)[None, :]
    return query.astype(BF16), key.astype(BF16)


def split3(values):
    high = values.astype(BF16)
    rest = values - high.astype(F32)
    middle = rest.astype(BF16)
    return high, middle, (rest - middle.astype(F32)).astype(BF16)


def rows_of(refs):
    return jnp.concatenate([ref[...] for ref in refs], axis=0)


def attend_kernel(parts, *refs):
    q_refs, k_refs, v_refs = refs[:parts], refs[parts : 2 * parts], refs[2 * parts : 3 * parts]
    fq_ref, fk_ref, pad_ref = refs[3 * parts : 3 * parts + 3]
    ctx_refs, (qa_ref, qb_ref) = refs[3 * parts + 3 : -2], refs[-2:]
    q = rows_of(q_refs) * BF16(HD**-0.5)
    k = rows_of(k_refs)
    v = rows_of(v_refs)
    block = q.shape[0]
    low = lax.broadcasted_iota(jnp.int32, q.shape, 1) < HD
    row = lax.broadcasted_iota(jnp.int32, (LANES, block), 0)
    upper = row < HD
    inner = row & (HD - 1)
    fq = fq_ref[...]
    fk = fk_ref[...]
    v_t = jnp.transpose(v)
    one = jnp.ones((), BF16)
    v_own = v_t.astype(F32)
    product = jnp.transpose(q.astype(F32) * k.astype(F32))
    padded = pad_ref[...] == 0
    outs, log_totals = [], []
    for head in range(2):
        first = head == 0
        q_head = jnp.where(low, q, fq) if first else jnp.where(low, fq, q)
        k_head = jnp.where(low, k, fk) if first else jnp.where(low, fk, k)
        v_head = jnp.where(upper, v_t, one) if first else jnp.where(upper, one, v_t)
        mine = upper if first else ~upper
        own = jnp.sum(product[head * HD : head * HD + HD], axis=0, keepdims=True)
        own = jnp.where(padded, own, -1e30)
        scores = dot(k_head, q_head, NT)
        top = jnp.maximum(jnp.max(scores, axis=0, keepdims=True), own)
        expo = jnp.exp(scores - top).astype(BF16)
        both = dot(v_head, expo) + jnp.exp(own - top) * jnp.where(mine, v_own, 1.0)
        total = both[HD : HD + 1] if first else both[0:1]
        outs.append(both / total)
        log_totals.append(split3(-(top + jnp.log(total))))
    context = jnp.transpose(jnp.where(upper, outs[0], outs[1])).astype(BF16)
    rows = block // parts
    for part, ctx_ref in enumerate(ctx_refs):
        ctx_ref[...] = context[part * rows : (part + 1) * rows]
    extra = jnp.zeros((LANES, block), F32)
    for at in range(3):
        piece = jnp.where(upper, log_totals[1][at].astype(F32), log_totals[0][at].astype(F32))
        extra = jnp.where(inner == 7 + at, piece, extra)
    fq = fq + jnp.transpose(extra).astype(BF16)
    qa_ref[...] = jnp.where(low, q, fq)
    qb_ref[...] = jnp.where(low, fq, q)


def attend(turn, qkv, fq, fk, pad):
    parts = len(qkv)
    rows, cols = qkv[0].shape[0], qkv[0].shape[1] // 3
    seq_len = parts * rows
    pairs = cols // LANES
    at = lambda which: [pl.BlockSpec((rows, LANES), lambda p: (0, which * pairs + p))] * parts
    tall = pl.BlockSpec((seq_len, LANES), lambda p: (0, p))
    part = pl.BlockSpec((rows, LANES), lambda p: (0, p))
    *ctx, qa, qb = call(
        turn,
        functools.partial(attend_kernel, parts),
        "attend",
        (pairs,),
        at(0) + at(1) + at(2) + [whole(fq), whole(fk), whole(pad)],
        [part] * parts + [tall] * 2,
        [shape((rows, pairs * LANES), BF16)] * parts + [shape((seq_len, pairs * LANES), BF16)] * 2,
        (*qkv, *qkv, *qkv, fq, fk, pad),
        4000 * seq_len * seq_len * pairs,
        40,
        stay=True,
    )
    return ctx, qa, qb


def attend_back_kernel(parts, qa_ref, qb_ref, fk_ref, pad_ref, *refs):
    *refs, out_ref = refs
    k, v, ctx, dctx = (rows_of(refs[at * parts : (at + 1) * parts]) for at in range(4))
    lane = lax.broadcasted_iota(jnp.int32, k.shape, 1)
    low = lane < HD
    inner = lane & (HD - 1)
    fk = fk_ref[...]
    k_own = k.astype(F32)
    dctx_f = dctx.astype(F32)
    product = dctx_f * ctx.astype(F32)
    product_v = dctx_f * v.astype(F32)
    padded = pad_ref[...] == 0
    one = jnp.ones((), BF16)
    zero = jnp.zeros((), BF16)
    dctx_t = jnp.transpose(dctx)
    dq, dk, dv = [], [], []
    for head in range(2):
        mine = low if head == 0 else ~low
        span = slice(head * HD, head * HD + HD)
        q_head = (qa_ref if head == 0 else qb_ref)[...]
        k_head = jnp.where(mine, k, fk)
        v_head = jnp.where(mine, v, one)
        delta = jnp.sum(jnp.where(mine, product, 0.0), axis=1, keepdims=True)
        high, middle, rest = split3(-delta)
        extra = jnp.where(inner == 0, high, jnp.where(inner == 1, middle, jnp.where(inner == 2, rest, zero)))
        weights = jnp.exp(dot(q_head, k_head, NT))
        d_raw = (weights * dot(jnp.where(mine, dctx, extra), v_head, NT)).astype(BF16)
        q_f = q_head.astype(F32)
        lifted = jnp.sum(jnp.where(~mine & (inner >= 7) & (inner < 10), q_f, 0.0), axis=1, keepdims=True)
        own = jnp.sum(jnp.where(mine, q_f * k_own, 0.0), axis=1, keepdims=True) + lifted
        w_own = jnp.where(padded, jnp.exp(jnp.where(padded, own, 0.0)), 0.0)
        d_own = w_own * (jnp.sum(jnp.where(mine, product_v, 0.0), axis=1, keepdims=True) - delta)
        dq.append(dot(d_raw, k) + d_own * k_own)
        dk.append((dot(jnp.transpose(q_head)[span], d_raw), d_own * q_f))
        dv.append((dot(dctx_t[span], weights.astype(BF16)), w_own * dctx_f))
    out_ref[0] = (jnp.where(low, dq[0], dq[1]) * HD**-0.5).astype(BF16)
    for at, parts in ((1, dk), (2, dv)):
        main = jnp.transpose(jnp.concatenate([parts[0][0], parts[1][0]], axis=0))
        out_ref[at] = (main + jnp.where(low, parts[0][1], parts[1][1])).astype(BF16)


def attend_back(turn, qa, qb, qkv, fk, pad, ctx, dctx, first, pairs):
    parts = len(qkv)
    rows, cols = qkv[0].shape[0], qkv[0].shape[1] // 3
    seq_len = parts * rows
    total = cols // LANES
    tall = pl.BlockSpec((seq_len, LANES), lambda p: (0, first + p))
    part = [pl.BlockSpec((rows, LANES), lambda p: (0, first + p))] * parts
    at = lambda which: [pl.BlockSpec((rows, LANES), lambda p: (0, which * total + first + p))] * parts
    return call(
        turn,
        functools.partial(attend_back_kernel, parts),
        "attend_back",
        (pairs,),
        [tall, tall, whole(fk), whole(pad)] + at(1) + at(2) + part + at(0),
        [pl.BlockSpec((3, seq_len, LANES), lambda p: (0, 0, p))],
        [shape((3, seq_len, pairs * LANES), BF16)],
        (qa, qb, fk, pad, *qkv, *qkv, *ctx, *dctx),
        6700 * seq_len * seq_len * pairs,
        44,
        stay=True,
        weight=0.5 if first == 0 else 0.1,
    )[0]


def feed_kernel(bits, counts, place, x_ref, gain_ref, g_ref, *refs):
    heads, groups, own = counts
    wo_refs, refs = refs[:heads], refs[heads:]
    ctx_refs, refs = refs[:groups], refs[groups:]
    (wi0_ref, wi1_ref, wf_ref), refs = refs[:3], refs[3:]
    deep_ref, out_ref, dnorm_ref, norm_t_ref, grad_t_ref = refs[:5]
    context = jnp.concatenate([ctx[...] for ctx in ctx_refs], axis=1)
    h1 = x_ref[...].astype(F32)
    at = 0
    for wo_ref in wo_refs:
        h1 = h1 + dot(context[:, at : at + wo_ref.shape[0]], wo_ref[...])
        at += wo_ref.shape[0]
    if own:
        h1_ref, joined_ref = refs[5:7]
        h1_ref[...] = h1
        for at in range(joined_ref.shape[0]):
            joined_ref[at] = context[:, at * joined_ref.shape[2] : (at + 1) * joined_ref.shape[2]]
    inverse = lax.rsqrt(jnp.mean(h1 * h1, axis=1, keepdims=True) + EPSILON)
    norm = (h1 * inverse * gain_ref[...]).astype(BF16)
    grad = g_ref[...]
    store_transposed(place, norm, norm_t_ref, bits[0])
    store_transposed(place, grad, grad_t_ref, bits[1])

    gate = dot(norm, wi0_ref[...])
    up = dot(norm, wi1_ref[...])
    d_hidden = dot(grad, wf_ref[...], NT)
    slope = 0.7978845608028654
    square = gate * gate
    curve = jnp.tanh(slope * gate * (1.0 + 0.044715 * square))
    half = 0.5 * (1.0 + curve)
    active = gate * half
    d_active = half + 0.5 * gate * (1.0 - curve * curve) * (slope + (3.0 * 0.044715 * slope) * square)
    hidden = (active * up).astype(BF16)
    d_gate = (d_hidden * up * d_active).astype(BF16)
    d_up = (d_hidden * active).astype(BF16)
    deep_ref[0] = d_gate
    deep_ref[1] = d_up
    deep_ref[2] = hidden
    dnorm_ref[...] = (dot(d_gate, wi0_ref[...], NT) + dot(d_up, wi1_ref[...], NT)).astype(BF16)
    out_ref[...] = dot(hidden, wf_ref[...]).astype(BF16)


def feed(turn, place, bits, x, gain, grad, wo_parts, contexts, weights, own):
    rows, width = x.shape
    units = weights[0].shape[1]
    block = min(256, rows)
    steps = rows // block
    columns = sum(array.shape[1] for array, _ in contexts)
    wide = pl.BlockSpec((block, width), lambda i: (i, 0))
    tall = pl.BlockSpec((width, block), lambda i: (0, i))
    ctx_specs = [
        pl.BlockSpec((block, array.shape[1]), functools.partial(lambda at, i: (at * steps + i, 0), at))
        for array, at in contexts
    ]
    out_specs = [pl.BlockSpec((3, block, units), lambda i: (0, i, 0)), wide, wide, tall, tall]
    out_shapes = (
        [shape((3, rows, units), BF16)]
        + [shape((rows, width), BF16)] * 2
        + [shape((width, rows), BF16)] * 2
    )
    if own:
        out_specs += [wide, pl.BlockSpec((columns // own, block, own), lambda i: (0, i, 0))]
        out_shapes += [shape((rows, width), F32), shape((columns // own, rows, own), BF16)]
    kernel = functools.partial(feed_kernel, bits, (len(wo_parts), len(contexts), own))
    return call(
        turn,
        kernel,
        "feed",
        (steps,),
        [SMEM_SPEC, wide, whole(gain), wide]
        + [whole(w) for w in wo_parts]
        + ctx_specs
        + [pl.BlockSpec(memory_space=pltpu.VMEM)] * 3,
        out_specs,
        out_shapes,
        (place, x, gain, grad, *wo_parts, *[array for array, _ in contexts], *weights),
        rows * width * (15 * units + 2.5 * columns),
        40,
        pinned=weights,
        stay=True,
    )


def middle_kernel(bits, heads, place, dn_ref, h1_ref, gain_ref, g_ref, *refs):
    wo_refs, refs = refs[:heads], refs[heads:]
    recv_refs, (dh_ref, dgain_ref, turned_ref, *dctx_refs) = refs[: -3 - heads], refs[-3 - heads :]
    d_norm = dn_ref[...].astype(F32)
    for recv in recv_refs:
        d_norm = d_norm + recv[...].astype(F32)
    h1 = h1_ref[...]
    inverse = lax.rsqrt(jnp.mean(h1 * h1, axis=1, keepdims=True) + EPSILON)
    normed = h1 * inverse
    scaled = gain_ref[...] * d_norm
    d_h1 = g_ref[...].astype(F32) + inverse * (
        scaled - normed * jnp.mean(scaled * normed, axis=1, keepdims=True)
    )
    dh_ref[...] = d_h1
    branch = d_h1.astype(BF16)
    for wo_ref, dctx_ref in zip(wo_refs, dctx_refs):
        dctx_ref[...] = dot(branch, wo_ref[...], NT).astype(BF16)
    store_transposed(place, branch, turned_ref, bits)

    @pl.when(pl.program_id(0) == 0)
    def _():
        dgain_ref[...] = jnp.zeros_like(dgain_ref)

    dgain_ref[...] += jnp.sum(d_norm * normed, axis=0, keepdims=True)


def middle(turn, place, bits, d_norm, received, h1, gain, grad, wo_parts):
    rows, width = h1.shape
    block = min(256, rows)
    heads = len(wo_parts)
    wide = pl.BlockSpec((block, width), lambda i: (i, 0))
    return call(
        turn,
        functools.partial(middle_kernel, bits, heads),
        "middle",
        (rows // block,),
        [SMEM_SPEC, wide, wide, whole(gain), wide] + [whole(w) for w in wo_parts] + [wide] * len(received),
        [wide, pl.BlockSpec((1, width), lambda i: (0, 0)), pl.BlockSpec((width, block), lambda i: (0, i))]
        + [pl.BlockSpec((block, w.shape[0]), lambda i: (i, 0)) for w in wo_parts],
        [shape((rows, width), F32), shape((1, width), F32), shape((width, rows), BF16)]
        + [shape((rows, w.shape[0]), BF16) for w in wo_parts],
        (place, d_norm, h1, gain, grad, *wo_parts, *received),
        2.5 * rows * width * sum(w.shape[0] for w in wo_parts),
        20,
        weight=0.1,
    )


def dnorm1(turn, x, grads, weights, part):
    rows, width = x.shape
    block = min(256, rows)
    steps = rows // block
    count = len(grads)

    def kernel(x_ref, *refs):
        grad_refs, w_refs, (dn_ref, dgain_ref) = refs[:count], refs[count:-2], refs[-2:]
        d_norm = None
        for group, g_ref in enumerate(grad_refs):
            size = g_ref.shape[2]
            for which, w_ref in enumerate(w_refs):
                term = dot(g_ref[which], w_ref[:, group * size : (group + 1) * size], NT)
                d_norm = term if d_norm is None else d_norm + term
        dn_ref[...] = d_norm.astype(BF16)
        x = x_ref[...].astype(F32)
        inverse = lax.rsqrt(jnp.mean(x * x, axis=1, keepdims=True) + EPSILON)

        @pl.when(pl.program_id(0) == 0)
        def _():
            dgain_ref[...] = jnp.zeros_like(dgain_ref)

        dgain_ref[...] += jnp.sum(d_norm * (x * inverse), axis=0, keepdims=True)

    wide = pl.BlockSpec((block, width), lambda i: (i, 0))
    return call(
        turn,
        kernel,
        "dnorm1",
        (steps,),
        [wide]
        + [pl.BlockSpec((3, block, g.shape[2]), lambda i: (0, part * steps + i, 0)) for g in grads]
        + [whole(w) for w in weights],
        [wide, pl.BlockSpec((1, width), lambda i: (0, 0))],
        [shape((rows, width), BF16), shape((1, width), F32)],
        (x, *grads, *weights),
        2.5 * rows * width * 3 * weights[0].shape[1],
        20,
    )


def last_kernel(dn_ref, x_ref, gain_ref, dh_ref, *rest):
    recv_refs, dx_ref = rest[:-1], rest[-1]
    d_norm = dn_ref[...].astype(F32)
    for recv in recv_refs:
        d_norm = d_norm + recv[...].astype(F32)
    x = x_ref[...].astype(F32)
    inverse = lax.rsqrt(jnp.mean(x * x, axis=1, keepdims=True) + EPSILON)
    normed = x * inverse
    scaled = gain_ref[...] * d_norm
    dx_ref[...] = dh_ref[...] + inverse * (
        scaled - normed * jnp.mean(scaled * normed, axis=1, keepdims=True)
    )


def last(turn, d_norm, received, x, gain, d_h1):
    rows, width = x.shape
    block = min(256, rows)
    wide = pl.BlockSpec((block, width), lambda i: (i, 0))
    return call(
        turn,
        last_kernel,
        "last",
        (rows // block,),
        [wide, wide, whole(gain), wide] + [wide] * len(received),
        [wide],
        [shape((rows, width), F32)],
        (d_norm, x, gain, d_h1, *received),
        100 * rows * width,
        20,
    )[0]


def weight_grads(turn, sides, start, received, joint=False, stay=False):
    count = sides[0][0][0].shape[0] // 2
    received = received or []
    cuts = 2 if received else 1
    lefts = [left for side in sides for left in side[0]]
    rights, right_specs, spans = [], [], []
    for lefts_of, rights_of, lowest, weights in sides:
        first = spans[-1][1] if spans else 0
        columns = rights_of[0][0].shape[2]
        spans.append((first, first + weights))
        for left, (right, at) in zip(lefts_of, rights_of):
            rights.append(right)
            right_specs.append(
                pl.BlockSpec(
                    (1, left.shape[1], columns),
                    functools.partial(
                        lambda f, n, low, at, w: (low + jnp.clip(w - f, 0, n - 1), at, 0),
                        first, weights, lowest, at,
                    ),
                )
            )

    wholes = [(0, spans[-1][1])] if joint else spans
    outputs = len(wholes)

    def kernel(*refs):
        left_refs = refs[: len(lefts)]
        right_refs = refs[len(lefts) : len(lefts) + len(rights)]
        recv_refs = refs[len(lefts) + len(rights) : len(refs) - cuts * outputs]
        out_refs = refs[len(refs) - cuts * outputs :]
        weight = pl.program_id(0)
        at = 0
        for side, (first, last) in enumerate(spans):

            @pl.when((weight >= first) & (weight < last))
            def _(side=side, at=at):
                out = 0 if joint else side
                total = recv_refs[out][...].astype(F32) if recv_refs else None
                for part in range(at, at + len(sides[side][0])):
                    term = dot(left_refs[part][...], right_refs[part][0])
                    total = term if total is None else total + term
                rows = count // cuts
                for cut in range(cuts):
                    out_refs[out * cuts + cut][...] = total[cut * rows : (cut + 1) * rows].astype(BF16)

            at += len(sides[side][0])

    widths = [side[1][0][0].shape[2] for side in sides][:outputs]

    def specs(rows):
        return [
            pl.BlockSpec(
                (rows, columns),
                functools.partial(lambda f, n, w: (0, jnp.clip(w - f, 0, n - 1)), first, last - first),
            )
            for columns, (first, last) in zip(widths, wholes)
        ]

    out_specs, out_shapes = [], []
    for spec, columns, (first, last) in zip(specs(count // cuts), widths, wholes):
        out_specs += [spec] * cuts
        out_shapes += [shape((count // cuts, (last - first) * columns), BF16)] * cuts
    outs = call(
        turn,
        kernel,
        "weight_grads",
        (spans[-1][1],),
        [pl.BlockSpec((count, left.shape[1]), lambda w: (start, 0)) for left in lefts]
        + right_specs
        + (specs(count) if received else []),
        out_specs,
        out_shapes,
        (*lefts, *rights, *received),
        2.5 * count * sum(side[3] * side[1][0][0].shape[2] * l.shape[1] for side in sides for l in side[0]),
        28,
        stay=stay,
    )
    return [tuple(outs[at : at + 2]) for at in range(0, len(outs), 2)] if received else outs


def add(left, right):
    return (left.astype(F32) + right.astype(F32)).astype(BF16)


def swap(array, bit):
    size = lax.axis_size("dp")
    return lax.ppermute(array, "dp", [(i, i ^ (1 << bit)) for i in range(size)])


def halve(turn, totals, arrived):
    outs = []
    arrived = turn.join(*arrived)
    for (_, kept), came in zip(totals, arrived):
        cut = kept.shape[0] // 2
        outs.append((add(kept[:cut], came[:cut]), add(kept[cut:], came[cut:])))
    flat = turn.join(*[part for pair in outs for part in pair])
    return list(zip(flat[::2], flat[1::2]))


def finish(totals, arrived):
    return [kept.astype(F32) + came.astype(F32) for (_, kept), came in zip(totals, arrived)]


def exchange(totals, orders, at):
    return [swap(send, order[at]) for (send, _), order in zip(totals, orders)]


def per_device(
    layer_in, seg_ids, pad_mask, wq, wk, wv, wo, wi0, wi1, wf, gain_attn, gain_ffn, out_grad
):
    dp, mp = lax.axis_size("dp"), lax.axis_size("mp")
    at_dp, at_mp = lax.axis_index("dp"), lax.axis_index("mp")
    bits = tuple(range(dp.bit_length() - 1))
    bits_other = bits[:1] + bits[2:3] + bits[1:2] + bits[3:]
    bits_wi = bits[:2] + bits[3:4] + bits[2:3] + bits[4:]
    place = jnp.stack([(at_dp >> bit) & 1 for bit in bits]).astype(jnp.int32)
    seq_len = seg_ids.shape[1]
    x = layer_in[0]
    grad = out_grad[0]
    rows, width = x.shape
    cols = wq.shape[1]
    gain_attn = gain_attn.reshape(1, width)
    gain_ffn = gain_ffn.reshape(1, width)

    def from_shift(array, shift):
        return lax.ppermute(array, "mp", [((d + shift) % mp, d) for d in range(mp)])

    def to_shift(array, shift):
        return lax.ppermute(array, "mp", [(d, (d + shift) % mp) for d in range(mp)])

    own_first = lambda a: jnp.roll(a[0], -at_mp * rows).astype(jnp.int32)
    seg, pad = own_first(seg_ids), own_first(pad_mask)
    fq, fk = mask_features(seg, pad)
    pad_row, pad_column = pad.reshape(1, seq_len), pad.reshape(seq_len, 1)
    turn = Turn()
    others = range(1, mp)

    piece = wo.shape[0] // dp
    wo_piece = lax.dynamic_slice_in_dim(wo, at_dp * piece, piece, 0)
    x, wo_piece = lax.optimization_barrier((x, wo_piece))
    wo_pieces = [from_shift(wo_piece, shift) for shift in others]
    x_parts = [x] + [from_shift(x, shift) for shift in others]

    qkv, norm1_t = [], []
    for part in range(mp):
        if part == 1:
            wo_parts = [wo]
            for got in turn.join(*wo_pieces):
                wo_parts.append(lax.all_gather(got, "dp", axis=0, tiled=True))
            grad, *x_parts[1:] = turn.join(grad, *x_parts[1:])
        got = project(turn, place, bits, x_parts[part], gain_attn, wq, wk, wv)
        qkv.append(got[0])
        norm1_t.append(got[1])
    g_parts = [grad] + [from_shift(grad, shift) for shift in others]

    total_pairs = cols // LANES
    group = max(1, total_pairs // 2)
    groups = [(first, group) for first in range(0, total_pairs, group)]

    ctx, qa, qb = attend(turn, qkv, fq, fk, pad_row)
    near = [from_shift(ctx[mp - shift], shift) for shift in others]
    weights = pin(turn, wi0, wi1, wf)
    far = [[from_shift(ctx[(part - shift) % mp], shift) for shift in others] for part in others]

    deep, norm2_t, grad_t, d_norm2, ffn_out = ([None] * mp for _ in range(5))
    for part in range(mp):
        contexts = [(array, 0) for array in [ctx[part], *(far[part - 1] if part else near)]]
        deep[part], ffn_out[part], d_norm2[part], norm2_t[part], grad_t[part], *kept = feed(
            turn, place, (bits_wi, bits_other), x_parts[part], gain_ffn, g_parts[part],
            wo_parts, contexts, weights, None if part else group * LANES,
        )
        if part == 0:
            h1, joined = kept
    dn_received = [to_shift(d_norm2[part], part) for part in others]
    *ffn_out[1:], last_received = lax.optimization_barrier((*ffn_out[1:], dn_received[-1]))
    dn_received[-1] = last_received
    ffn_received = [to_shift(ffn_out[part], part) for part in others]

    deep = pin(turn, *deep)
    units = wi0.shape[1]
    cuts = [(0, 2)] if units % LANES == 0 else [(0, 1), (1, 1)]
    rights = [(array, 0) for array in deep]
    ffn_sides = [(norm2_t, rights, low, count) for low, count in cuts] + [(grad_t, rights, 2, 1)]
    ffn_orders = [bits_wi] * len(cuts) + [bits_other]
    sent = weight_grads(turn, ffn_sides, 0, None)
    held = lax.optimization_barrier((*sent, *dn_received))
    sent, dn_received = held[: len(sent)], list(held[len(sent) :])
    arrived = [swap(array, order[0]) for array, order in zip(sent, ffn_orders)]

    d_h1, dgain_ffn, branch_t, *d_ctx_all = middle(
        turn, place, bits, d_norm2[0], dn_received, h1, gain_ffn, grad, wo_parts
    )
    d_ctx = [d_ctx_all[0]] + [from_shift(d_ctx_all[mp - shift], shift) for shift in others]

    ffn_totals = weight_grads(turn, ffn_sides, 1, arrived)
    ffn_arrived = exchange(ffn_totals, ffn_orders, 1)

    stages = len(bits)

    def advance_ffn(at):
        nonlocal ffn_totals, ffn_arrived
        if at < stages:
            ffn_totals = halve(turn, ffn_totals, ffn_arrived)
            ffn_arrived = exchange(ffn_totals, ffn_orders, at)

    def advance(index, at):
        if at < stages:
            totals[index] = halve(turn, totals[index], waiting[index])
            waiting[index] = exchange(totals[index], [bits], at)

    grads, totals, waiting = [], [], []
    tail = len(groups) - 1
    dn_parts = [None] * mp
    for index, (first, pairs) in enumerate(groups):
        got = attend_back(turn, qa, qb, qkv, fk, pad_column, ctx, d_ctx, first, pairs)
        grads.append(got)
        sides = [(norm1_t, [(got, part) for part in range(mp)], 0, 3)]
        if index == 0:
            sides.append(([branch_t], [(joined, 0)], 0, joined.shape[0]))
        sent = weight_grads(turn, sides, 0, None, True)
        arrived = [swap(array, bits[0]) for array in sent]
        if index == 0:
            advance_ffn(2)
            if not tail:
                advance_ffn(3)
        if index == tail:
            if tail:
                advance(0, 2)
                advance_ffn(3)
            for part in others:
                dn_parts[part] = dnorm1(turn, x_parts[part], grads, (wq, wk, wv), part)
            dn1_received = [to_shift(dn_parts[part][0], part) for part in others]
        totals.append(weight_grads(turn, sides, 1, arrived, True))
        waiting.append(exchange(totals[index], [bits], 1))
    dn_parts[0] = dnorm1(turn, x_parts[0], grads, (wq, wk, wv), 0)
    dgains = jnp.concatenate([sum(p[1] for p in dn_parts), dgain_ffn], axis=0)
    gains_arrived = swap(dgains, bits[0])
    if tail:
        advance(0, 3)

    layer_out = h1 + ffn_out[0].astype(F32)
    for received in turn.join(*ffn_received):
        layer_out = layer_out + received.astype(F32)
    layer_out = layer_out.astype(BF16)

    for at in range(2, stages):
        gains_came, *waiting[tail] = turn.join(gains_arrived, *waiting[tail])
        dgains = dgains + gains_came
        gains_arrived = swap(dgains, bits[at - 1])
        advance(tail, at)
    for at in range(4, stages):
        if tail:
            advance(0, at)
        advance_ffn(at)
    dgains = dgains + turn.join(gains_arrived)[0]
    gains_arrived = swap(dgains, bits[-1])
    wide = group * LANES
    ffn_totals = finish(ffn_totals, turn.join(*ffn_arrived))
    wo_grad = finish(totals[0], turn.join(*waiting[0]))[0][:, 3 * wide :]
    wo_arrived = [
        from_shift(wo_grad[:, (mp - shift) * cols : (mp - shift + 1) * cols].astype(BF16), shift)
        for shift in others
    ]
    dgains = dgains + turn.join(gains_arrived)[0]
    gains_parts = [dgains] + [from_shift(dgains, shift) for shift in others]
    d_x = last(turn, dn_parts[0][0], dn1_received, x, gain_attn, d_h1)
    totals = [finish(total, turn.join(*came)) for total, came in zip(totals, waiting)]
    d_wo = wo_grad[:, :cols]
    for array in turn.join(*wo_arrived):
        d_wo = d_wo + array.astype(F32)
    dgains = sum(turn.join(*gains_parts)) + turn.token.astype(F32)
    d_wi, d_wf = jnp.concatenate(ffn_totals[:-1], axis=1), ffn_totals[-1]
    pieces = [total[0][:, : 3 * wide].reshape(-1, 3, wide) for total in totals]
    d_wq, d_wk, d_wv = (
        jnp.concatenate([piece[:, which] for piece in pieces], axis=1) for which in range(3)
    )
    return (
        layer_out[None],
        d_x[None],
        d_wq,
        d_wk,
        d_wv,
        d_wo.T,
        d_wi[:, :units],
        d_wi[:, units:],
        d_wf.T,
        dgains[0],
        dgains[1],
    )


def solution(mesh):
    return jax.shard_map(
        per_device,
        mesh=mesh,
        in_specs=(
            P("dp", "mp", None),
            P("dp", None),
            P("dp", None),
            P(None, "mp"),
            P(None, "mp"),
            P(None, "mp"),
            P("mp", None),
            P(None, "mp"),
            P(None, "mp"),
            P("mp", None),
            P(),
            P(),
            P("dp", "mp", None),
        ),
        out_specs=(
            P("dp", "mp", None),
            P("dp", "mp", None),
            P("dp", "mp"),
            P("dp", "mp"),
            P("dp", "mp"),
            P("mp", "dp"),
            P("dp", "mp"),
            P("dp", "mp"),
            P("mp", "dp"),
            P(),
            P(),
        ),
        check_vma=False,
    )
```

```python
import functools

import jax
import jax.numpy as jnp
from jax import lax
from jax.experimental import pallas as pl
from jax.experimental.pallas import tpu as pltpu
from jax.sharding import PartitionSpec as P

HD = 64
LANES = 128
EPSILON = 1e-06
BIG = 2.0**30
F32 = jnp.float32
BF16 = jnp.bfloat16
NN = (((1,), (0,)), ((), ()))
NT = (((1,), (1,)), ((), ()))
MIB = 1 << 20
IN_HBM = ("attend", "weight_grads", "middle", "feed", "project", "attend_back", "dnorm1",)


def dot(lhs, rhs, dims=NN):
    return lax.dot_general(lhs, rhs, dims, preferred_element_type=F32)


class Turn:
    def __init__(self):
        self.token = jnp.zeros((1,), jnp.int32)

    def join(self, *arrays):
        self.token, *arrays = lax.optimization_barrier((self.token, *arrays))
        return arrays


def call(turn, kernel, name, grid, in_specs, out_specs, out_shape, args, flops, vmem, scratch=(), stay=False, pinned=(), weight=0.1):
    token_at = len(args) + len(out_shape)

    if stay:
        large = lambda a: a.size * a.dtype.itemsize > MIB // 4 and not any(a is b for b in pinned)
        args = [pltpu.with_memory_space_constraint(a, pltpu.HBM) if large(a) else a for a in args]

    placed = [
        pltpu.HBM(o.shape, o.dtype) if o.size * o.dtype.itemsize > MIB // 4 and name in IN_HBM else o for o in out_shape
    ]

    def with_token(token_ref, *refs):
        @pl.when(functools.reduce(lambda a, b: a & b, [pl.program_id(d) == 0 for d in range(len(grid))]))
        def _():
            refs[token_at][0] = 0

        kernel(*refs[:token_at], *refs[token_at + 1 :])

    *outs, turn.token = pl.pallas_call(
        with_token,
        grid=grid,
        in_specs=[pl.BlockSpec(memory_space=pl.ANY), *in_specs],
        out_specs=[*out_specs, pl.BlockSpec(memory_space=pltpu.SMEM)],
        out_shape=[*placed, shape((1,), jnp.int32)],
        scratch_shapes=list(scratch),
        compiler_params=pltpu.CompilerParams(vmem_limit_bytes=vmem * MIB),
        cost_estimate=pl.CostEstimate(
            flops=int(weight * flops),
            bytes_accessed=int(weight * sum(a.size * a.dtype.itemsize for a in (*args, *out_shape))),
            transcendentals=0,
        ),
        name=name,
    )(turn.token, *args)
    return outs


def pin(turn, *arrays):
    count = len(arrays)
    anywhere = pl.BlockSpec(memory_space=pl.ANY)

    def kernel(*refs):
        refs[-1][0] = 0

    *outs, turn.token = pl.pallas_call(
        kernel,
        in_specs=[anywhere] * (count + 1),
        out_specs=[anywhere] * count + [pl.BlockSpec(memory_space=pltpu.SMEM)],
        out_shape=[pltpu.VMEM(a.shape, a.dtype) for a in arrays] + [shape((1,), jnp.int32)],
        input_output_aliases={at + 1: at for at in range(count)},
        compiler_params=pltpu.CompilerParams(vmem_limit_bytes=4 * MIB),
        name="pin",
    )(turn.token, *[pltpu.with_memory_space_constraint(a, pltpu.VMEM) for a in arrays])
    return outs


def whole(array):
    zeros = (0,) * array.ndim
    return pl.BlockSpec(array.shape, lambda *_: zeros)


def shape(dims, dtype):
    return jax.ShapeDtypeStruct(dims, dtype)


SMEM_SPEC = pl.BlockSpec(memory_space=pltpu.SMEM)


def store_transposed(place_ref, values, out_ref, bits):
    turned = jnp.transpose(values)
    count = len(bits)
    rows = turned.shape[0] >> count
    for index in range(1 << count):
        target = 0
        for at, bit in enumerate(bits):
            own = 1 - (place_ref[bit] ^ ((index >> bit) & 1))
            target = target + own * (1 << (count - 1 - at))
        out_ref[pl.ds(pl.multiple_of(target * rows, rows), rows), :] = turned[
            index * rows : (index + 1) * rows
        ]


def project_kernel(bits, place, x_ref, gain_ref, wq_ref, wk_ref, wv_ref, qkv_ref, turned_ref):
    x = x_ref[...].astype(F32)
    inverse = lax.rsqrt(jnp.mean(x * x, axis=1, keepdims=True) + EPSILON)
    norm = (x * inverse * gain_ref[...]).astype(BF16)
    cols = wq_ref.shape[1]
    for index, weight in enumerate((wq_ref, wk_ref, wv_ref)):
        qkv_ref[:, index * cols : (index + 1) * cols] = dot(norm, weight[...]).astype(BF16)
    store_transposed(place, norm, turned_ref, bits)


def project(turn, place, bits, x, gain, wq, wk, wv):
    rows, width = x.shape
    block = min(256, rows)
    cols = wq.shape[1]
    return call(
        turn,
        functools.partial(project_kernel, bits),
        "project",
        (rows // block,),
        [
            SMEM_SPEC,
            pl.BlockSpec((block, width), lambda i: (i, 0)),
            whole(gain),
            whole(wq),
            whole(wk),
            whole(wv),
        ],
        [
            pl.BlockSpec((block, 3 * cols), lambda i: (i, 0)),
            pl.BlockSpec((width, block), lambda i: (0, i)),
        ],
        [shape((rows, 3 * cols), BF16), shape((width, rows), BF16)],
        (place, x, gain, wq, wk, wv),
        2.5 * rows * width * 3 * cols,
        20,
        stay=True,
    )


def mask_features(seg, pad):
    lane = jnp.arange(LANES) % HD
    same = seg[:, None] == lane[None, :]
    seg_lane = (lane < 6)[None, :]
    pad_lane = (lane == 6)[None, :]
    query = jnp.where(seg_lane & ~same, -BIG, 0.0) + jnp.where(pad_lane, -BIG, 0.0)
    key = jnp.where(seg_lane & same, 1.0, 0.0)
    key = key + jnp.where(pad_lane & (pad[:, None] == 0), 1.0, 0.0)
    key = key + jnp.where((lane >= 7) & (lane < 10), 1.0, 0.0)[None, :]
    return query.astype(BF16), key.astype(BF16)


def split3(values):
    high = values.astype(BF16)
    rest = values - high.astype(F32)
    middle = rest.astype(BF16)
    return high, middle, (rest - middle.astype(F32)).astype(BF16)


def rows_of(refs):
    return jnp.concatenate([ref[...] for ref in refs], axis=0)


def attend_kernel(parts, *refs):
    q_refs, k_refs, v_refs = refs[:parts], refs[parts : 2 * parts], refs[2 * parts : 3 * parts]
    fq_ref, fk_ref, pad_ref = refs[3 * parts : 3 * parts + 3]
    ctx_refs, (qa_ref, qb_ref) = refs[3 * parts + 3 : -2], refs[-2:]
    q = rows_of(q_refs) * BF16(HD**-0.5)
    k = rows_of(k_refs)
    v = rows_of(v_refs)
    block = q.shape[0]
    low = lax.broadcasted_iota(jnp.int32, q.shape, 1) < HD
    row = lax.broadcasted_iota(jnp.int32, (LANES, block), 0)
    upper = row < HD
    inner = row & (HD - 1)
    fq = fq_ref[...]
    fk = fk_ref[...]
    v_t = jnp.transpose(v)
    one = jnp.ones((), BF16)
    v_own = v_t.astype(F32)
    product = jnp.transpose(q.astype(F32) * k.astype(F32))
    padded = pad_ref[...] == 0
    outs, log_totals = [], []
    for head in range(2):
        first = head == 0
        q_head = jnp.where(low, q, fq) if first else jnp.where(low, fq, q)
        k_head = jnp.where(low, k, fk) if first else jnp.where(low, fk, k)
        v_head = jnp.where(upper, v_t, one) if first else jnp.where(upper, one, v_t)
        mine = upper if first else ~upper
        own = jnp.sum(product[head * HD : head * HD + HD], axis=0, keepdims=True)
        own = jnp.where(padded, own, -1e30)
        scores = dot(k_head, q_head, NT)
        top = jnp.maximum(jnp.max(scores, axis=0, keepdims=True), own)
        expo = jnp.exp(scores - top).astype(BF16)
        both = dot(v_head, expo) + jnp.exp(own - top) * jnp.where(mine, v_own, 1.0)
        total = both[HD : HD + 1] if first else both[0:1]
        outs.append(both / total)
        log_totals.append(split3(-(top + jnp.log(total))))
    context = jnp.transpose(jnp.where(upper, outs[0], outs[1])).astype(BF16)
    rows = block // parts
    for part, ctx_ref in enumerate(ctx_refs):
        ctx_ref[...] = context[part * rows : (part + 1) * rows]
    extra = jnp.zeros((LANES, block), F32)
    for at in range(3):
        piece = jnp.where(upper, log_totals[1][at].astype(F32), log_totals[0][at].astype(F32))
        extra = jnp.where(inner == 7 + at, piece, extra)
    fq = fq + jnp.transpose(extra).astype(BF16)
    qa_ref[...] = jnp.where(low, q, fq)
    qb_ref[...] = jnp.where(low, fq, q)


def attend(turn, qkv, fq, fk, pad):
    parts = len(qkv)
    rows, cols = qkv[0].shape[0], qkv[0].shape[1] // 3
    seq_len = parts * rows
    pairs = cols // LANES
    at = lambda which: [pl.BlockSpec((rows, LANES), lambda p: (0, which * pairs + p))] * parts
    tall = pl.BlockSpec((seq_len, LANES), lambda p: (0, p))
    part = pl.BlockSpec((rows, LANES), lambda p: (0, p))
    *ctx, qa, qb = call(
        turn,
        functools.partial(attend_kernel, parts),
        "attend",
        (pairs,),
        at(0) + at(1) + at(2) + [whole(fq), whole(fk), whole(pad)],
        [part] * parts + [tall] * 2,
        [shape((rows, pairs * LANES), BF16)] * parts + [shape((seq_len, pairs * LANES), BF16)] * 2,
        (*qkv, *qkv, *qkv, fq, fk, pad),
        4000 * seq_len * seq_len * pairs,
        40,
        stay=True,
    )
    return ctx, qa, qb


def attend_back_kernel(parts, qa_ref, qb_ref, fk_ref, pad_ref, *refs):
    *refs, out_ref = refs
    k, v, ctx, dctx = (rows_of(refs[at * parts : (at + 1) * parts]) for at in range(4))
    lane = lax.broadcasted_iota(jnp.int32, k.shape, 1)
    low = lane < HD
    inner = lane & (HD - 1)
    fk = fk_ref[...]
    k_own = k.astype(F32)
    dctx_f = dctx.astype(F32)
    product = dctx_f * ctx.astype(F32)
    product_v = dctx_f * v.astype(F32)
    padded = pad_ref[...] == 0
    one = jnp.ones((), BF16)
    zero = jnp.zeros((), BF16)
    dctx_t = jnp.transpose(dctx)
    dq, dk, dv = [], [], []
    for head in range(2):
        mine = low if head == 0 else ~low
        span = slice(head * HD, head * HD + HD)
        q_head = (qa_ref if head == 0 else qb_ref)[...]
        k_head = jnp.where(mine, k, fk)
        v_head = jnp.where(mine, v, one)
        delta = jnp.sum(jnp.where(mine, product, 0.0), axis=1, keepdims=True)
        high, middle, rest = split3(-delta)
        extra = jnp.where(inner == 0, high, jnp.where(inner == 1, middle, jnp.where(inner == 2, rest, zero)))
        weights = jnp.exp(dot(q_head, k_head, NT))
        d_raw = (weights * dot(jnp.where(mine, dctx, extra), v_head, NT)).astype(BF16)
        q_f = q_head.astype(F32)
        lifted = jnp.sum(jnp.where(~mine & (inner >= 7) & (inner < 10), q_f, 0.0), axis=1, keepdims=True)
        own = jnp.sum(jnp.where(mine, q_f * k_own, 0.0), axis=1, keepdims=True) + lifted
        w_own = jnp.where(padded, jnp.exp(jnp.where(padded, own, 0.0)), 0.0)
        d_own = w_own * (jnp.sum(jnp.where(mine, product_v, 0.0), axis=1, keepdims=True) - delta)
        dq.append(dot(d_raw, k) + d_own * k_own)
        dk.append((dot(jnp.transpose(q_head)[span], d_raw), d_own * q_f))
        dv.append((dot(dctx_t[span], weights.astype(BF16)), w_own * dctx_f))
    out_ref[0] = (jnp.where(low, dq[0], dq[1]) * HD**-0.5).astype(BF16)
    for at, parts in ((1, dk), (2, dv)):
        main = jnp.transpose(jnp.concatenate([parts[0][0], parts[1][0]], axis=0))
        out_ref[at] = (main + jnp.where(low, parts[0][1], parts[1][1])).astype(BF16)


def attend_back(turn, qa, qb, qkv, fk, pad, ctx, dctx, first, pairs):
    parts = len(qkv)
    rows, cols = qkv[0].shape[0], qkv[0].shape[1] // 3
    seq_len = parts * rows
    total = cols // LANES
    tall = pl.BlockSpec((seq_len, LANES), lambda p: (0, first + p))
    part = [pl.BlockSpec((rows, LANES), lambda p: (0, first + p))] * parts
    at = lambda which: [pl.BlockSpec((rows, LANES), lambda p: (0, which * total + first + p))] * parts
    return call(
        turn,
        functools.partial(attend_back_kernel, parts),
        "attend_back",
        (pairs,),
        [tall, tall, whole(fk), whole(pad)] + at(1) + at(2) + part + at(0),
        [pl.BlockSpec((3, seq_len, LANES), lambda p: (0, 0, p))],
        [shape((3, seq_len, pairs * LANES), BF16)],
        (qa, qb, fk, pad, *qkv, *qkv, *ctx, *dctx),
        6700 * seq_len * seq_len * pairs,
        44,
        stay=True,
        weight=0.5 if first == 0 else 0.1,
    )[0]


def feed_kernel(bits, counts, place, x_ref, gain_ref, g_ref, *refs):
    heads, groups, own = counts
    wo_refs, refs = refs[:heads], refs[heads:]
    ctx_refs, refs = refs[:groups], refs[groups:]
    (wi0_ref, wi1_ref, wf_ref), refs = refs[:3], refs[3:]
    deep_ref, out_ref, dnorm_ref, norm_t_ref, grad_t_ref = refs[:5]
    context = jnp.concatenate([ctx[...] for ctx in ctx_refs], axis=1)
    h1 = x_ref[...].astype(F32)
    at = 0
    for wo_ref in wo_refs:
        h1 = h1 + dot(context[:, at : at + wo_ref.shape[0]], wo_ref[...])
        at += wo_ref.shape[0]
    if own:
        h1_ref, joined_ref = refs[5:7]
        h1_ref[...] = h1
        for at in range(joined_ref.shape[0]):
            joined_ref[at] = context[:, at * joined_ref.shape[2] : (at + 1) * joined_ref.shape[2]]
    inverse = lax.rsqrt(jnp.mean(h1 * h1, axis=1, keepdims=True) + EPSILON)
    norm = (h1 * inverse * gain_ref[...]).astype(BF16)
    grad = g_ref[...]
    store_transposed(place, norm, norm_t_ref, bits[0])
    store_transposed(place, grad, grad_t_ref, bits[1])

    gate = dot(norm, wi0_ref[...])
    up = dot(norm, wi1_ref[...])
    d_hidden = dot(grad, wf_ref[...], NT)
    slope = 0.7978845608028654
    square = gate * gate
    curve = jnp.tanh(slope * gate * (1.0 + 0.044715 * square))
    half = 0.5 * (1.0 + curve)
    active = gate * half
    d_active = half + 0.5 * gate * (1.0 - curve * curve) * (slope + (3.0 * 0.044715 * slope) * square)
    hidden = (active * up).astype(BF16)
    d_gate = (d_hidden * up * d_active).astype(BF16)
    d_up = (d_hidden * active).astype(BF16)
    deep_ref[0] = d_gate
    deep_ref[1] = d_up
    deep_ref[2] = hidden
    dnorm_ref[...] = (dot(d_gate, wi0_ref[...], NT) + dot(d_up, wi1_ref[...], NT)).astype(BF16)
    out_ref[...] = dot(hidden, wf_ref[...]).astype(BF16)


def feed(turn, place, bits, x, gain, grad, wo_parts, contexts, weights, own):
    rows, width = x.shape
    units = weights[0].shape[1]
    block = min(256, rows)
    steps = rows // block
    columns = sum(array.shape[1] for array, _ in contexts)
    wide = pl.BlockSpec((block, width), lambda i: (i, 0))
    tall = pl.BlockSpec((width, block), lambda i: (0, i))
    ctx_specs = [
        pl.BlockSpec((block, array.shape[1]), functools.partial(lambda at, i: (at * steps + i, 0), at))
        for array, at in contexts
    ]
    out_specs = [pl.BlockSpec((3, block, units), lambda i: (0, i, 0)), wide, wide, tall, tall]
    out_shapes = (
        [shape((3, rows, units), BF16)]
        + [shape((rows, width), BF16)] * 2
        + [shape((width, rows), BF16)] * 2
    )
    if own:
        out_specs += [wide, pl.BlockSpec((columns // own, block, own), lambda i: (0, i, 0))]
        out_shapes += [shape((rows, width), F32), shape((columns // own, rows, own), BF16)]
    kernel = functools.partial(feed_kernel, bits, (len(wo_parts), len(contexts), own))
    return call(
        turn,
        kernel,
        "feed",
        (steps,),
        [SMEM_SPEC, wide, whole(gain), wide]
        + [whole(w) for w in wo_parts]
        + ctx_specs
        + [pl.BlockSpec(memory_space=pltpu.VMEM)] * 3,
        out_specs,
        out_shapes,
        (place, x, gain, grad, *wo_parts, *[array for array, _ in contexts], *weights),
        rows * width * (15 * units + 2.5 * columns),
        40,
        pinned=weights,
        stay=True,
    )


def middle_kernel(bits, heads, place, dn_ref, h1_ref, gain_ref, g_ref, *refs):
    wo_refs, refs = refs[:heads], refs[heads:]
    recv_refs, (dh_ref, dgain_ref, turned_ref, *dctx_refs) = refs[: -3 - heads], refs[-3 - heads :]
    d_norm = dn_ref[...].astype(F32)
    for recv in recv_refs:
        d_norm = d_norm + recv[...].astype(F32)
    h1 = h1_ref[...]
    inverse = lax.rsqrt(jnp.mean(h1 * h1, axis=1, keepdims=True) + EPSILON)
    normed = h1 * inverse
    scaled = gain_ref[...] * d_norm
    d_h1 = g_ref[...].astype(F32) + inverse * (
        scaled - normed * jnp.mean(scaled * normed, axis=1, keepdims=True)
    )
    dh_ref[...] = d_h1
    branch = d_h1.astype(BF16)
    for wo_ref, dctx_ref in zip(wo_refs, dctx_refs):
        dctx_ref[...] = dot(branch, wo_ref[...], NT).astype(BF16)
    store_transposed(place, branch, turned_ref, bits)

    @pl.when(pl.program_id(0) == 0)
    def _():
        dgain_ref[...] = jnp.zeros_like(dgain_ref)

    dgain_ref[...] += jnp.sum(d_norm * normed, axis=0, keepdims=True)


def middle(turn, place, bits, d_norm, received, h1, gain, grad, wo_parts):
    rows, width = h1.shape
    block = min(256, rows)
    heads = len(wo_parts)
    wide = pl.BlockSpec((block, width), lambda i: (i, 0))
    return call(
        turn,
        functools.partial(middle_kernel, bits, heads),
        "middle",
        (rows // block,),
        [SMEM_SPEC, wide, wide, whole(gain), wide] + [whole(w) for w in wo_parts] + [wide] * len(received),
        [wide, pl.BlockSpec((1, width), lambda i: (0, 0)), pl.BlockSpec((width, block), lambda i: (0, i))]
        + [pl.BlockSpec((block, w.shape[0]), lambda i: (i, 0)) for w in wo_parts],
        [shape((rows, width), F32), shape((1, width), F32), shape((width, rows), BF16)]
        + [shape((rows, w.shape[0]), BF16) for w in wo_parts],
        (place, d_norm, h1, gain, grad, *wo_parts, *received),
        2.5 * rows * width * sum(w.shape[0] for w in wo_parts),
        20,
        weight=0.1,
    )


def dnorm1(turn, x, grads, weights, part):
    rows, width = x.shape
    block = min(256, rows)
    steps = rows // block
    count = len(grads)

    def kernel(x_ref, *refs):
        grad_refs, w_refs, (dn_ref, dgain_ref) = refs[:count], refs[count:-2], refs[-2:]
        d_norm = None
        for group, g_ref in enumerate(grad_refs):
            size = g_ref.shape[2]
            for which, w_ref in enumerate(w_refs):
                term = dot(g_ref[which], w_ref[:, group * size : (group + 1) * size], NT)
                d_norm = term if d_norm is None else d_norm + term
        dn_ref[...] = d_norm.astype(BF16)
        x = x_ref[...].astype(F32)
        inverse = lax.rsqrt(jnp.mean(x * x, axis=1, keepdims=True) + EPSILON)

        @pl.when(pl.program_id(0) == 0)
        def _():
            dgain_ref[...] = jnp.zeros_like(dgain_ref)

        dgain_ref[...] += jnp.sum(d_norm * (x * inverse), axis=0, keepdims=True)

    wide = pl.BlockSpec((block, width), lambda i: (i, 0))
    return call(
        turn,
        kernel,
        "dnorm1",
        (steps,),
        [wide]
        + [pl.BlockSpec((3, block, g.shape[2]), lambda i: (0, part * steps + i, 0)) for g in grads]
        + [whole(w) for w in weights],
        [wide, pl.BlockSpec((1, width), lambda i: (0, 0))],
        [shape((rows, width), BF16), shape((1, width), F32)],
        (x, *grads, *weights),
        2.5 * rows * width * 3 * weights[0].shape[1],
        20,
    )


def last_kernel(dn_ref, x_ref, gain_ref, dh_ref, *rest):
    recv_refs, dx_ref = rest[:-1], rest[-1]
    d_norm = dn_ref[...].astype(F32)
    for recv in recv_refs:
        d_norm = d_norm + recv[...].astype(F32)
    x = x_ref[...].astype(F32)
    inverse = lax.rsqrt(jnp.mean(x * x, axis=1, keepdims=True) + EPSILON)
    normed = x * inverse
    scaled = gain_ref[...] * d_norm
    dx_ref[...] = dh_ref[...] + inverse * (
        scaled - normed * jnp.mean(scaled * normed, axis=1, keepdims=True)
    )


def last(turn, d_norm, received, x, gain, d_h1):
    rows, width = x.shape
    block = min(256, rows)
    wide = pl.BlockSpec((block, width), lambda i: (i, 0))
    return call(
        turn,
        last_kernel,
        "last",
        (rows // block,),
        [wide, wide, whole(gain), wide] + [wide] * len(received),
        [wide],
        [shape((rows, width), F32)],
        (d_norm, x, gain, d_h1, *received),
        100 * rows * width,
        20,
    )[0]


def weight_grads(turn, sides, start, received, joint=False, stay=False):
    count = sides[0][0][0].shape[0] // 2
    received = received or []
    cuts = 2 if received else 1
    lefts = [left for side in sides for left in side[0]]
    rights, right_specs, spans = [], [], []
    for lefts_of, rights_of, lowest, weights in sides:
        first = spans[-1][1] if spans else 0
        columns = rights_of[0][0].shape[2]
        spans.append((first, first + weights))
        for left, (right, at) in zip(lefts_of, rights_of):
            rights.append(right)
            right_specs.append(
                pl.BlockSpec(
                    (1, left.shape[1], columns),
                    functools.partial(
                        lambda f, n, low, at, w: (low + jnp.clip(w - f, 0, n - 1), at, 0),
                        first, weights, lowest, at,
                    ),
                )
            )

    wholes = [(0, spans[-1][1])] if joint else spans
    outputs = len(wholes)

    def kernel(*refs):
        left_refs = refs[: len(lefts)]
        right_refs = refs[len(lefts) : len(lefts) + len(rights)]
        recv_refs = refs[len(lefts) + len(rights) : len(refs) - cuts * outputs]
        out_refs = refs[len(refs) - cuts * outputs :]
        weight = pl.program_id(0)
        at = 0
        for side, (first, last) in enumerate(spans):

            @pl.when((weight >= first) & (weight < last))
            def _(side=side, at=at):
                out = 0 if joint else side
                total = recv_refs[out][...].astype(F32) if recv_refs else None
                for part in range(at, at + len(sides[side][0])):
                    term = dot(left_refs[part][...], right_refs[part][0])
                    total = term if total is None else total + term
                rows = count // cuts
                for cut in range(cuts):
                    out_refs[out * cuts + cut][...] = total[cut * rows : (cut + 1) * rows].astype(BF16)

            at += len(sides[side][0])

    widths = [side[1][0][0].shape[2] for side in sides][:outputs]

    def specs(rows):
        return [
            pl.BlockSpec(
                (rows, columns),
                functools.partial(lambda f, n, w: (0, jnp.clip(w - f, 0, n - 1)), first, last - first),
            )
            for columns, (first, last) in zip(widths, wholes)
        ]

    out_specs, out_shapes = [], []
    for spec, columns, (first, last) in zip(specs(count // cuts), widths, wholes):
        out_specs += [spec] * cuts
        out_shapes += [shape((count // cuts, (last - first) * columns), BF16)] * cuts
    outs = call(
        turn,
        kernel,
        "weight_grads",
        (spans[-1][1],),
        [pl.BlockSpec((count, left.shape[1]), lambda w: (start, 0)) for left in lefts]
        + right_specs
        + (specs(count) if received else []),
        out_specs,
        out_shapes,
        (*lefts, *rights, *received),
        2.5 * count * sum(side[3] * side[1][0][0].shape[2] * l.shape[1] for side in sides for l in side[0]),
        28,
        stay=stay,
    )
    return [tuple(outs[at : at + 2]) for at in range(0, len(outs), 2)] if received else outs


def add(left, right):
    return (left.astype(F32) + right.astype(F32)).astype(BF16)


def swap(array, bit):
    size = lax.axis_size("dp")
    return lax.ppermute(array, "dp", [(i, i ^ (1 << bit)) for i in range(size)])


def halve(turn, totals, arrived):
    outs = []
    arrived = turn.join(*arrived)
    for (_, kept), came in zip(totals, arrived):
        cut = kept.shape[0] // 2
        outs.append((add(kept[:cut], came[:cut]), add(kept[cut:], came[cut:])))
    flat = turn.join(*[part for pair in outs for part in pair])
    return list(zip(flat[::2], flat[1::2]))


def finish(totals, arrived):
    return [kept.astype(F32) + came.astype(F32) for (_, kept), came in zip(totals, arrived)]


def exchange(totals, orders, at):
    return [swap(send, order[at]) for (send, _), order in zip(totals, orders)]


def per_device(
    layer_in, seg_ids, pad_mask, wq, wk, wv, wo, wi0, wi1, wf, gain_attn, gain_ffn, out_grad
):
    dp, mp = lax.axis_size("dp"), lax.axis_size("mp")
    at_dp, at_mp = lax.axis_index("dp"), lax.axis_index("mp")
    bits = tuple(range(dp.bit_length() - 1))
    bits_other = bits[:1] + bits[2:3] + bits[1:2] + bits[3:]
    bits_wi = bits[:2] + bits[3:4] + bits[2:3] + bits[4:]
    place = jnp.stack([(at_dp >> bit) & 1 for bit in bits]).astype(jnp.int32)
    seq_len = seg_ids.shape[1]
    x = layer_in[0]
    grad = out_grad[0]
    rows, width = x.shape
    cols = wq.shape[1]
    gain_attn = gain_attn.reshape(1, width)
    gain_ffn = gain_ffn.reshape(1, width)

    def from_shift(array, shift):
        return lax.ppermute(array, "mp", [((d + shift) % mp, d) for d in range(mp)])

    def to_shift(array, shift):
        return lax.ppermute(array, "mp", [(d, (d + shift) % mp) for d in range(mp)])

    own_first = lambda a: jnp.roll(a[0], -at_mp * rows).astype(jnp.int32)
    seg, pad = own_first(seg_ids), own_first(pad_mask)
    fq, fk = mask_features(seg, pad)
    pad_row, pad_column = pad.reshape(1, seq_len), pad.reshape(seq_len, 1)
    turn = Turn()
    others = range(1, mp)

    piece = wo.shape[0] // dp
    wo_piece = lax.dynamic_slice_in_dim(wo, at_dp * piece, piece, 0)
    x, wo_piece = lax.optimization_barrier((x, wo_piece))
    wo_pieces = [from_shift(wo_piece, shift) for shift in others]
    x_parts = [x] + [from_shift(x, shift) for shift in others]

    qkv, norm1_t = [], []
    for part in range(mp):
        if part == 1:
            wo_parts = [wo]
            for got in turn.join(*wo_pieces):
                wo_parts.append(lax.all_gather(got, "dp", axis=0, tiled=True))
            grad, *x_parts[1:] = turn.join(grad, *x_parts[1:])
        got = project(turn, place, bits_wi, x_parts[part], gain_attn, wq, wk, wv)
        qkv.append(got[0])
        norm1_t.append(got[1])
    g_parts = [grad] + [from_shift(grad, shift) for shift in others]

    total_pairs = cols // LANES
    group = max(1, total_pairs // 2)
    groups = [(first, group) for first in range(0, total_pairs, group)]

    ctx, qa, qb = attend(turn, qkv, fq, fk, pad_row)
    near = [from_shift(ctx[mp - shift], shift) for shift in others]
    weights = pin(turn, wi0, wi1, wf)
    far = [[from_shift(ctx[(part - shift) % mp], shift) for shift in others] for part in others]

    deep, norm2_t, grad_t, d_norm2, ffn_out = ([None] * mp for _ in range(5))
    for part in range(mp):
        contexts = [(array, 0) for array in [ctx[part], *(far[part - 1] if part else near)]]
        deep[part], ffn_out[part], d_norm2[part], norm2_t[part], grad_t[part], *kept = feed(
            turn, place, (bits_wi, bits_other), x_parts[part], gain_ffn, g_parts[part],
            wo_parts, contexts, weights, None if part else group * LANES,
        )
        if part == 0:
            h1, joined = kept
    dn_received = [to_shift(d_norm2[part], part) for part in others]
    *ffn_out[1:], last_received = lax.optimization_barrier((*ffn_out[1:], dn_received[-1]))
    dn_received[-1] = last_received
    ffn_received = [to_shift(ffn_out[part], part) for part in others]

    deep = pin(turn, *deep)
    units = wi0.shape[1]
    cuts = [(0, 2)] if units % LANES == 0 else [(0, 1), (1, 1)]
    rights = [(array, 0) for array in deep]
    ffn_sides = [(norm2_t, rights, low, count) for low, count in cuts] + [(grad_t, rights, 2, 1)]
    ffn_orders = [bits_wi] * len(cuts) + [bits_other]
    sent = weight_grads(turn, ffn_sides, 0, None)
    held = lax.optimization_barrier((*sent, *dn_received))
    sent, dn_received = held[: len(sent)], list(held[len(sent) :])
    arrived = [swap(array, order[0]) for array, order in zip(sent, ffn_orders)]

    d_h1, dgain_ffn, branch_t, *d_ctx_all = middle(
        turn, place, bits_wi, d_norm2[0], dn_received, h1, gain_ffn, grad, wo_parts
    )
    d_ctx = [d_ctx_all[0]] + [from_shift(d_ctx_all[mp - shift], shift) for shift in others]

    ffn_totals = weight_grads(turn, ffn_sides, 1, arrived)
    ffn_arrived = exchange(ffn_totals, ffn_orders, 1)

    stages = len(bits)

    def advance_ffn(at):
        nonlocal ffn_totals, ffn_arrived
        if at < stages:
            ffn_totals = halve(turn, ffn_totals, ffn_arrived)
            ffn_arrived = exchange(ffn_totals, ffn_orders, at)

    def advance(index, at):
        if at < stages:
            totals[index] = halve(turn, totals[index], waiting[index])
            waiting[index] = exchange(totals[index], [bits_wi], at)

    grads, totals, waiting = [], [], []
    tail = len(groups) - 1
    dn_parts = [None] * mp
    for index, (first, pairs) in enumerate(groups):
        got = attend_back(turn, qa, qb, qkv, fk, pad_column, ctx, d_ctx, first, pairs)
        grads.append(got)
        sides = [(norm1_t, [(got, part) for part in range(mp)], 0, 3)]
        if index == 0:
            sides.append(([branch_t], [(joined, 0)], 0, joined.shape[0]))
        sent = weight_grads(turn, sides, 0, None, True)
        arrived = [swap(array, bits[0]) for array in sent]
        if index == 0:
            advance_ffn(2)
            if not tail:
                advance_ffn(3)
        if index == tail:
            if tail:
                advance(0, 2)
                advance_ffn(3)
            for part in others:
                dn_parts[part] = dnorm1(turn, x_parts[part], grads, (wq, wk, wv), part)
            dn1_received = [to_shift(dn_parts[part][0], part) for part in others]
        totals.append(weight_grads(turn, sides, 1, arrived, True))
        waiting.append(exchange(totals[index], [bits_wi], 1))
    dn_parts[0] = dnorm1(turn, x_parts[0], grads, (wq, wk, wv), 0)
    dgains = jnp.concatenate([sum(p[1] for p in dn_parts), dgain_ffn], axis=0)
    gains_arrived = swap(dgains, bits[0])
    if tail:
        advance(0, 3)

    layer_out = h1 + ffn_out[0].astype(F32)
    for received in turn.join(*ffn_received):
        layer_out = layer_out + received.astype(F32)
    layer_out = layer_out.astype(BF16)

    for at in range(2, stages):
        gains_came, *waiting[tail] = turn.join(gains_arrived, *waiting[tail])
        dgains = dgains + gains_came
        gains_arrived = swap(dgains, bits[at - 1])
        advance(tail, at)
    for at in range(4, stages):
        if tail:
            advance(0, at)
        advance_ffn(at)
    dgains = dgains + turn.join(gains_arrived)[0]
    gains_arrived = swap(dgains, bits[-1])
    wide = group * LANES
    ffn_totals = finish(ffn_totals, turn.join(*ffn_arrived))
    wo_grad = finish(totals[0], turn.join(*waiting[0]))[0][:, 3 * wide :]
    wo_arrived = [
        from_shift(wo_grad[:, (mp - shift) * cols : (mp - shift + 1) * cols].astype(BF16), shift)
        for shift in others
    ]
    dgains = dgains + turn.join(gains_arrived)[0]
    gains_parts = [dgains] + [from_shift(dgains, shift) for shift in others]
    d_x = last(turn, dn_parts[0][0], dn1_received, x, gain_attn, d_h1)
    totals = [finish(total, turn.join(*came)) for total, came in zip(totals, waiting)]
    d_wo = wo_grad[:, :cols]
    for array in turn.join(*wo_arrived):
        d_wo = d_wo + array.astype(F32)
    dgains = sum(turn.join(*gains_parts)) + turn.token.astype(F32)
    d_wi, d_wf = jnp.concatenate(ffn_totals[:-1], axis=1), ffn_totals[-1]
    pieces = [total[0][:, : 3 * wide].reshape(-1, 3, wide) for total in totals]
    d_wq, d_wk, d_wv = (
        jnp.concatenate([piece[:, which] for piece in pieces], axis=1) for which in range(3)
    )
    return (
        layer_out[None],
        d_x[None],
        d_wq,
        d_wk,
        d_wv,
        d_wo.T,
        d_wi[:, :units],
        d_wi[:, units:],
        d_wf.T,
        dgains[0],
        dgains[1],
    )


def solution(mesh):
    return jax.shard_map(
        per_device,
        mesh=mesh,
        in_specs=(
            P("dp", "mp", None),
            P("dp", None),
            P("dp", None),
            P(None, "mp"),
            P(None, "mp"),
            P(None, "mp"),
            P("mp", None),
            P(None, "mp"),
            P(None, "mp"),
            P("mp", None),
            P(),
            P(),
            P("dp", "mp", None),
        ),
        out_specs=(
            P("dp", "mp", None),
            P("dp", "mp", None),
            P("dp", "mp"),
            P("dp", "mp"),
            P("dp", "mp"),
            P("mp", "dp"),
            P("dp", "mp"),
            P("dp", "mp"),
            P("mp", "dp"),
            P(),
            P(),
        ),
        check_vma=False,
    )
```
